512 devices in a mesh: replica: 64 (over z, y), tensor: 8 (over x, core).
Axes of the slice: x: 4, y: 8, z: 8, core: 2. Of those that a mesh axis runs over, the one named last changes fastest.
Arguments:
- mamba_in: bfloat16 [1024, 3, 2, 8192], P('replica', None, None, 'tensor'), may hold values from -6 to 6
- queries: bfloat16 [1024, 3, 8, 1024], P('replica', None, 'tensor'), may hold values from -400 to 400
- new_kv: bfloat16 [1024, 3, 8, 256], P('replica', None, 'tensor'), may hold values from -6 to 6
- ssm_state: float32 [1024, 16, 8192], P('replica', None, 'tensor'), may hold values from -4 to 4
- kv_cache: bfloat16 [1024, 16, 8, 256], P('replica', None, 'tensor'), may hold values from -16 to 16
- lengths: int32 [1024], P('replica'), may hold values from 1 to 16, 8192 in all
- destination: int32 [1024, 1], P('replica'), may hold values from 0 to 63; in each aligned block of 16 rows (0 to 15, 16 to 31, ...) no two rows name the same one
- xproj_w: bfloat16 [8192, 544], P('tensor'), may hold values from -0.0625 to 0.0625
- dtproj_w: bfloat16 [512, 8192], P(None, 'tensor'), may hold values from -0.25 to 0.25
- dt_bias: float32 [8192], P('tensor'), may hold values from -5 to -2
- a_log: float32 [16, 8192], P(None, 'tensor'), may hold values from 0 to 2.77
- d_skip: float32 [8192], P('tensor'), may hold values from 0.1 to 1.9
Outputs:
- mixed: bfloat16 [4096, 3, 8192], P('replica', None, 'tensor')
- attended: bfloat16 [4096, 3, 8, 1024], P('replica', None, 'tensor')
- moved_state: bfloat16 [4096, 16, 8192], P('replica', None, 'tensor')
- moved_pages: bfloat16 [4096, 19, 8, 256], P('replica', None, 'tensor')
The draws below stay inside these ranges and needn't reach their ends.
Inputs may be any that keep to these rules, and one draw needn't show every extreme that they name: `destination`: among the 16 rows of one replica, no replica is named more than 1 times; every replica takes some row.
All inputs are finite; a program needn't handle non-finite values. No bound on the sum of `lengths` on one device may be relied on, other than what follows from the above.
Results may differ from the reference program's by a relative error of at most 0.0075.
Values may be sent and summed in bfloat16 or wider, within the bound.
A program may use at most 64 MiB of HBM per device.

```python
import math
import jax
import jax.numpy as jnp
import numpy as np
from jax import lax

CH = 8192
DSTATE = 16
DT_RANK = 512
XP = 544
KV_HEADS = 8
GROUP = 8
HD = 128
STEPS = 3
ROWS = 16
CTX = 16
PAGES = 19
CAP = 1
ROWS_ALL = 1024
SLOTS = 4096
N_REPLICA = 64


def shared_keys(key):
    return jax.random.normal(key, (ROWS_ALL, CTX, KV_HEADS, HD), jnp.float32)


def draw_kv_cache(key, part):
    cache_keys = shared_keys(key)
    key = jax.random.fold_in(key, 11)
    cache_vals = jax.random.normal(key, (ROWS_ALL, CTX, KV_HEADS, HD), jnp.float32)
    return jnp.concatenate([cache_keys, cache_vals], axis=-1).astype(jnp.bfloat16)


def draw_queries(key, part):
    key = jax.random.fold_in(key, 12)
    base_draw = jax.random.normal(key, (ROWS_ALL, STEPS, KV_HEADS, GROUP * HD), jnp.float32)
    return base_draw.astype(jnp.bfloat16)


def block_levels(stream_key, dims, cuts, low, largest):
    loudness, own = 1.0, jax.random.fold_in(stream_key, 6)
    for dim, shards_of in cuts:
        steps = jnp.exp(jax.random.uniform(jax.random.fold_in(own, dim), (shards_of,), jnp.float32, low / len(cuts), largest / len(cuts)))
        loudness = loudness * jnp.repeat(steps, dims[dim] // shards_of).reshape([-1 if axis == dim else 1 for axis in range(len(dims))])
    return loudness


def profile(amount, total, most, slope):
    loads = [(1 << 20) // math.isqrt(rank ** slope) + 1 for rank in range(2, amount + 1)]
    rest, given = total - most - (amount - 1), [1] * (amount - 1)
    while rest > 0:
        candidates = [i for i in range(amount - 1) if given[i] < most]
        pool, budget = sum([loads[i] for i in candidates]), rest
        for i in candidates:
            more = min(most - given[i], max(1, budget * loads[i] // pool), rest)
            given[i] = given[i] + more
            rest = rest - more
    return np.array([most] + given)


def ragged_sizes(key, count, total, limit, skew):
    if count == 2:
        one = jax.random.randint(key, (), max(1, total - limit), min(limit, total - 1) + 1)
        return jnp.stack([one, total - one])
    sizes = jnp.asarray(profile(count, total, limit, skew), jnp.int32)
    twos = (count - 1) // 2
    giver, receiver = sizes[1:1 + 2 * twos:2], sizes[2:2 + 2 * twos:2]
    margin = jnp.minimum(giver - 1, limit - receiver)
    moved = jax.random.randint(jax.random.fold_in(key, 1), (twos,), 0, 1 << 20) % (margin + 1)
    sizes = sizes.at[1:1 + 2 * twos:2].set(giver - moved).at[2:2 + 2 * twos:2].set(receiver + moved)
    return sizes[jax.random.permutation(jax.random.fold_in(key, 2), count)]


def shared_out(key, own, number, rows, amount, top, reach, skew):
    order = jax.random.permutation(key, amount)
    heavy_load, common = shares(amount, rows * top, reach, skew, True), shares(amount, rows * top, reach, skew, False)
    places = jnp.arange(amount)

    def named(sizes, offset_by):
        used = int((sizes > 0).sum())
        fixed = max(1, used // 4)
        shifted = fixed + (places - fixed + offset_by * (used - fixed)) % max(1, amount - fixed)
        return jnp.zeros((amount,), jnp.int32).at[order[jnp.where(places < fixed, places, shifted)]].set(jnp.asarray(sizes, jnp.int32))

    sizes = jnp.where(number % 4 == 0, named(heavy_load, number // 4), named(common, number - number // 4 - 1))
    mixed = jax.random.permutation(jax.random.fold_in(own, 3), amount)
    giver, taker = mixed[0:amount // 2 * 2:2], mixed[1:amount // 2 * 2:2]
    margin = jnp.minimum(sizes[giver] - 1, reach - sizes[taker]) // 2
    margin = jnp.where((giver == order[0]) | (taker == order[0]) | (sizes[taker] == 0), 0, jnp.maximum(margin, 0))
    shifted = jax.random.randint(jax.random.fold_in(own, 4), (amount // 2,), 0, 1 << 20) % (margin + 1)
    sizes = sizes.at[giver].add(-shifted).at[taker].add(shifted)
    members = jnp.searchsorted(jnp.cumsum(sizes), jnp.arange(rows * top), side="right").astype(jnp.int32)
    grid = members.reshape(top, rows).T
    grid = grid[jax.random.permutation(jax.random.fold_in(own, 1), rows)]
    offset_by = jax.random.randint(jax.random.fold_in(own, 2), (rows, 1), 0, top)
    return jnp.take_along_axis(grid, (jnp.arange(top)[None, :] + offset_by) % top, axis=1)


def shares(amount, total, limit, lean, full):
    loads = [(1 << 20) // math.isqrt(grade ** lean) + 1 for grade in range(1, amount + 1)]
    largest = limit if full else min(limit, max(-(-total // amount), total * loads[0] // sum(loads)))
    least = 1 if total - largest >= amount - 1 else 0
    given, rest = [largest] + [least] * (amount - 1), total - largest - least * (amount - 1)
    while rest > 0:
        candidates = [i for i in range(1, amount) if given[i] < largest] or [i for i in range(1, amount) if given[i] < limit]
        whole, left = sum([loads[i] for i in candidates]), rest
        for i in candidates:
            more = min(limit - given[i], max(1, left * loads[i] // whole), rest)
            given[i] = given[i] + more
            rest = rest - more
    return np.array(given)


def bell_draw(rng, shape, width, reach, shards=(), kind=jnp.bfloat16):
    loudness = block_levels(rng, shape, shards, -0.22, 0.18) if shards else 1.0
    result = jax.random.normal(rng, shape, jnp.float32) * width * loudness
    return jnp.minimum(jnp.maximum(result, -reach), reach).astype(kind)


def setup_inputs(seed: int = 0) -> dict:
    seeds = jax.random.split(jax.random.key(seed), 13)
    mamba_in = bell_draw(seeds[0], (ROWS_ALL, STEPS, 2, CH), 1.0, 6.0, ((0, 64), (3, 8)))
    queries = draw_queries(jax.random.fold_in(seeds[12], 71), 0)
    new_kv = bell_draw(seeds[2], (ROWS_ALL, STEPS, KV_HEADS, 2 * HD), 1.0, 6.0, ((0, 64), (2, 8)))
    ssm_state = bell_draw(seeds[3], (ROWS_ALL, DSTATE, CH), 0.5, 4.0, ((0, 64), (2, 8)), jnp.float32)
    kv_cache = draw_kv_cache(jax.random.fold_in(seeds[12], 71), 0)
    lengths = ragged_sizes(seeds[5], ROWS_ALL, ROWS_ALL * CTX // 2, CTX, 2).astype(jnp.int32)
    destination_keys = jax.random.split(jax.random.fold_in(seeds[6], 1), ROWS_ALL // ROWS)
    destination_turns = jax.random.permutation(jax.random.fold_in(seeds[6], 3), ROWS_ALL // ROWS)
    destination = jax.vmap(lambda own, number: shared_out(jax.random.fold_in(seeds[6], 2), own, number, ROWS, N_REPLICA, 1, CAP, 2))(destination_keys, destination_turns).reshape((ROWS_ALL, 1))
    xproj_w = bell_draw(seeds[7], (CH, XP), CH ** -0.5, 0.0625, ((0, 8),))
    dtproj_w = bell_draw(seeds[8], (DT_RANK, CH), DT_RANK ** -0.5, 0.25, ((1, 8),))
    dt_bias = jnp.clip(-5.0 + 3.0 * jax.random.uniform(seeds[9], (CH,), jnp.float32) ** block_levels(seeds[9], (CH,), ((0, 8),), -0.2, 0.2), -5.0, -2.0)
    a_log = jnp.clip(2.77 * jax.random.uniform(seeds[10], (DSTATE, CH), jnp.float32) ** block_levels(seeds[10], (DSTATE, CH), ((1, 8),), -0.2, 0.2), 0.0, 2.77)
    d_skip = jnp.clip(1.0 + 0.18 * jax.random.normal(seeds[11], (CH,), jnp.float32), 0.1, 1.9)
    return dict(mamba_in=mamba_in, queries=queries, new_kv=new_kv, ssm_state=ssm_state, kv_cache=kv_cache, lengths=lengths, destination=destination, xproj_w=xproj_w, dtproj_w=dtproj_w, dt_bias=dt_bias, a_log=a_log, d_skip=d_skip)


def extend_pages(kv_pages, new_kv, lengths):
    row_count = kv_pages.shape[0]
    step_count = new_kv.shape[1]
    padding = jnp.zeros((row_count, step_count) + kv_pages.shape[2:], kv_pages.dtype)
    grown = jnp.concatenate([kv_pages, padding], axis=1)
    position = jnp.arange(grown.shape[1], dtype=jnp.int32)[None, :]
    for offset in range(step_count):
        hit = (position == (lengths[:, None] + offset))[:, :, None, None]
        grown = jnp.where(hit, new_kv[:, offset][:, None], grown)
    return grown


def decode_rows(mamba_rows, queries, new_kv, ssm_carry, kv_pages, lengths, xproj_w, dtproj_w, dt_bias, a_log, d_skip):
    slot_count = mamba_rows.shape[0]
    decay_rate = -jnp.exp(a_log)
    score_scale = HD ** -0.5
    cache_keys = kv_pages[..., :HD].astype(jnp.float32)
    cache_vals = kv_pages[..., HD:].astype(jnp.float32)
    fresh_keys = new_kv[..., :HD].astype(jnp.float32)
    fresh_vals = new_kv[..., HD:].astype(jnp.float32)
    cache_mask = (jnp.arange(CTX, dtype=jnp.int32)[None, :] < lengths[:, None])[:, None, None, :]
    mixed_steps = []
    attended_steps = []
    for step_index in range(STEPS):
        x_in = mamba_rows[:, step_index, 0]
        z_in = mamba_rows[:, step_index, 1]
        projected = jnp.dot(x_in, xproj_w, preferred_element_type=jnp.float32)
        low_rank = projected[:, :DT_RANK].astype(jnp.bfloat16)
        b_vector = projected[:, DT_RANK:DT_RANK + DSTATE]
        c_vector = projected[:, DT_RANK + DSTATE:]
        step_size = jax.nn.softplus(jnp.dot(low_rank, dtproj_w, preferred_element_type=jnp.float32) + dt_bias)
        x_float = x_in.astype(jnp.float32)
        ssm_carry = jnp.exp(step_size[:, None, :] * decay_rate[None]) * ssm_carry + b_vector[:, :, None] * (step_size * x_float)[:, None, :]
        readout = jnp.einsum("nsc,ns->nc", ssm_carry, c_vector, precision=lax.Precision.HIGHEST) + d_skip * x_float
        mixed_steps.append((readout * jax.nn.silu(z_in.astype(jnp.float32))).astype(jnp.bfloat16))
        query = queries[:, step_index].reshape(slot_count, KV_HEADS, GROUP, HD).astype(jnp.float32)
        cache_scores = jnp.einsum("nhgd,nkhd->nhgk", query, cache_keys) * score_scale
        fresh_scores = jnp.einsum("nhgd,nkhd->nhgk", query, fresh_keys) * score_scale
        fresh_mask = (jnp.arange(STEPS) <= step_index)[None, None, None, :]
        row_max = jnp.maximum(jnp.max(jnp.where(cache_mask, cache_scores, -1e30), axis=-1), jnp.max(jnp.where(fresh_mask, fresh_scores, -1e30), axis=-1))
        cache_exp = jnp.where(cache_mask, jnp.exp(cache_scores - row_max[..., None]), 0.0)
        fresh_exp = jnp.where(fresh_mask, jnp.exp(fresh_scores - row_max[..., None]), 0.0)
        denominator = jnp.sum(cache_exp, axis=-1) + jnp.sum(fresh_exp, axis=-1)
        cache_weights = lax.optimization_barrier((cache_exp / denominator[..., None]).astype(jnp.bfloat16)).astype(jnp.float32)
        fresh_weights = lax.optimization_barrier((fresh_exp / denominator[..., None]).astype(jnp.bfloat16)).astype(jnp.float32)
        summed = jnp.einsum("nhgk,nkhd->nhgd", cache_weights, cache_vals) + jnp.einsum("nhgk,nkhd->nhgd", fresh_weights, fresh_vals)
        attended_steps.append(summed.reshape(slot_count, KV_HEADS, GROUP * HD).astype(jnp.bfloat16))
    grown = extend_pages(kv_pages, new_kv, lengths)
    return jnp.stack(mixed_steps, axis=1), jnp.stack(attended_steps, axis=1), ssm_carry.astype(jnp.bfloat16), grown


def reference(mamba_in, queries, new_kv, ssm_state, kv_cache, lengths, destination, xproj_w, dtproj_w, dt_bias, a_log, d_skip):
    def split_rows(array):
        return array.reshape((N_REPLICA, ROWS) + array.shape[1:])

    def one_block(pieces):
        return decode_rows(pieces[0], pieces[1], pieces[2], pieces[3], pieces[4], pieces[5], xproj_w, dtproj_w, dt_bias, a_log, d_skip)

    def join_rows(array):
        return array.reshape((ROWS_ALL,) + array.shape[2:])

    blocks = tuple(split_rows(array) for array in (mamba_in, queries, new_kv, ssm_state, kv_cache, lengths))
    mixed_rows, attended_rows, state_rows, page_rows = lax.map(one_block, blocks)
    mixed_rows = join_rows(mixed_rows)
    attended_rows = join_rows(attended_rows)
    state_rows = join_rows(state_rows)
    page_rows = join_rows(page_rows)
    targets = destination[:, 0].astype(jnp.int32)
    target_blocks = targets.reshape(N_REPLICA, ROWS)
    earlier = jnp.arange(ROWS, dtype=jnp.int32)[None, :] < jnp.arange(ROWS, dtype=jnp.int32)[:, None]
    same = target_blocks[:, :, None] == target_blocks[:, None, :]
    rank = jnp.sum((same & earlier[None]).astype(jnp.int32), axis=2).reshape(ROWS_ALL).astype(jnp.int32)
    source_replica = jnp.arange(ROWS_ALL, dtype=jnp.int32) // ROWS
    slot_index = (targets * (N_REPLICA * CAP) + source_replica * CAP + rank).astype(jnp.int32)
    mixed = jnp.zeros((SLOTS, STEPS, CH), jnp.bfloat16).at[slot_index].set(mixed_rows)
    attended = jnp.zeros((SLOTS, STEPS, KV_HEADS, GROUP * HD), jnp.bfloat16).at[slot_index].set(attended_rows)
    moved_state = jnp.zeros((SLOTS, DSTATE, CH), jnp.bfloat16).at[slot_index].set(state_rows)
    moved_pages = jnp.zeros((SLOTS, PAGES, KV_HEADS, 2 * HD), jnp.bfloat16).at[slot_index].set(page_rows)
    return mixed, attended, moved_state, moved_pages
```

```python
import jax
import jax.numpy as jnp
from jax import lax
from jax.sharding import PartitionSpec as P


def place_rows(source_rows, chosen, present):
    gathered = jnp.take(source_rows, chosen, axis=0)
    keeper = present.reshape((present.shape[0],) + (1,) * (source_rows.ndim - 1))
    return jnp.where(keeper, gathered, jnp.zeros_like(gathered))


def extend_pages(kv_pages, new_kv, lengths):
    row_count = kv_pages.shape[0]
    step_count = new_kv.shape[1]
    padding = jnp.zeros((row_count, step_count) + kv_pages.shape[2:], kv_pages.dtype)
    grown = jnp.concatenate([kv_pages, padding], axis=1)
    position = jnp.arange(grown.shape[1], dtype=jnp.int32)[None, :]
    for offset in range(step_count):
        hit = (position == lengths[:, None] + offset)[:, :, None, None]
        grown = jnp.where(hit, new_kv[:, offset][:, None], grown)
    return grown


def sending_rows(destination, peer_count):
    row_count = destination.shape[0]
    capacity = (row_count + peer_count - 1) // peer_count
    targets = destination[:, 0]
    row_ids = jnp.arange(row_count, dtype=jnp.int32)
    earlier = row_ids[None, :] < row_ids[:, None]
    same = targets[:, None] == targets[None, :]
    rank = jnp.sum((same & earlier).astype(jnp.int32), axis=1)
    send_slot = targets * capacity + rank
    slot_ids = jnp.arange(peer_count * capacity, dtype=jnp.int32)
    matches = send_slot[None, :] == slot_ids[:, None]
    return jnp.sum(jnp.where(matches, row_ids[None, :], 0), axis=1), jnp.any(matches, axis=1)


def attend(queries, new_kv, kv_cache, lengths):
    rows, steps, _, query_width = queries.shape
    context = kv_cache.shape[1]
    width = kv_cache.shape[3] // 2
    group = query_width // width
    query = queries.reshape(rows, steps * group, width)
    pages = jnp.concatenate([kv_cache[:, :, 0], new_kv[:, :, 0]], axis=1)
    scores = jnp.einsum(
        "nqd,nkd->nqk", query, pages[..., :width], preferred_element_type=jnp.float32
    ) * (width ** (-0.5))
    key_id = jnp.arange(context + steps, dtype=jnp.int32)
    step_id = jnp.arange(steps * group, dtype=jnp.int32) // group
    live = jnp.where(
        (key_id < context)[None, None, :],
        key_id[None, None, :] < lengths[:, None, None],
        (key_id[None, :] - context <= step_id[:, None])[None],
    )
    top = jnp.max(jnp.where(live, scores, -1e30), axis=-1, keepdims=True)
    raised = jnp.where(live, jnp.exp(scores - top), 0.0)
    weights = (raised / jnp.sum(raised, axis=-1, keepdims=True)).astype(jnp.bfloat16)
    summed = jnp.einsum(
        "nqk,nkd->nqd", weights, pages[..., width:], preferred_element_type=jnp.float32
    )
    return summed.astype(jnp.bfloat16).reshape(rows, steps, query_width)


def scan_state(mamba_in, ssm_state, xproj_w, dtproj_w, dt_bias, a_log, d_skip):
    rows, steps, _, width = mamba_in.shape
    low_width = dtproj_w.shape[0]
    state_size = a_log.shape[0]
    x_in = mamba_in[:, :, 0].reshape(rows * steps, width)
    projected = lax.psum(jnp.dot(x_in, xproj_w, preferred_element_type=jnp.float32), "tensor")
    low_rank = projected[:, :low_width].astype(jnp.bfloat16)
    step_size = jax.nn.softplus(
        jnp.dot(low_rank, dtproj_w, preferred_element_type=jnp.float32) + dt_bias
    ).reshape(rows, steps, width)
    b_all = projected[:, low_width : low_width + state_size].reshape(rows, steps, state_size)
    c_all = projected[:, low_width + state_size :].reshape(rows, steps, state_size)
    decay_rate = -jnp.exp(a_log)
    carry = ssm_state
    mixed = []
    for step in range(steps):
        x_float = mamba_in[:, step, 0].astype(jnp.float32)
        z_float = mamba_in[:, step, 1].astype(jnp.float32)
        size = step_size[:, step]
        carry = (
            jnp.exp(size[:, None, :] * decay_rate[None]) * carry
            + b_all[:, step, :, None] * (size * x_float)[:, None, :]
        )
        readout = jnp.sum(carry * c_all[:, step, :, None], axis=1) + d_skip * x_float
        mixed.append((readout * jax.nn.silu(z_float)).astype(jnp.bfloat16))
    return jnp.stack(mixed, axis=1), carry.astype(jnp.bfloat16)


def exchange(rows):
    return lax.all_to_all(rows, "replica", split_axis=0, concat_axis=0, tiled=True)


def per_device(
    mamba_in,
    queries,
    new_kv,
    ssm_state,
    kv_cache,
    lengths,
    destination,
    xproj_w,
    dtproj_w,
    dt_bias,
    a_log,
    d_skip,
):
    chosen, present = sending_rows(destination, lax.axis_size("replica"))
    rows, steps, _, width = mamba_in.shape
    state_size = a_log.shape[0]
    slots = chosen.shape[0]
    attended = attend(queries, new_kv, kv_cache, lengths)
    grown = extend_pages(kv_cache, new_kv, lengths)
    query_width = queries.shape[3]
    attended_size = steps * query_width
    early = jnp.concatenate(
        [attended.reshape(rows, attended_size), grown.reshape(rows, -1)], axis=1
    ).reshape(rows, 16, -1)
    early = exchange(place_rows(early, chosen, present)).reshape(slots, -1)
    mixed, state = scan_state(mamba_in, ssm_state, xproj_w, dtproj_w, dt_bias, a_log, d_skip)
    late = jnp.concatenate([state, mixed.reshape(rows, state_size, -1)], axis=2)
    late = exchange(place_rows(late, chosen, present))
    return (
        late[:, :, width:].reshape(slots, steps, width),
        early[:, :attended_size].reshape(slots, steps, 1, query_width),
        late[:, :, :width],
        early[:, attended_size:].reshape((slots,) + grown.shape[1:]),
    )


def solution(mesh):
    placed = (
        P("replica", None, None, "tensor"),
        P("replica", None, "tensor", None),
        P("replica", None, "tensor", None),
        P("replica", None, "tensor"),
        P("replica", None, "tensor", None),
        P("replica"),
        P("replica", None),
        P("tensor", None),
        P(None, "tensor"),
        P("tensor"),
        P(None, "tensor"),
        P("tensor"),
    )
    return jax.shard_map(
        per_device,
        mesh=mesh,
        in_specs=placed,
        out_specs=(
            P("replica", None, "tensor"),
            P("replica", None, "tensor", None),
            P("replica", None, "tensor"),
            P("replica", None, "tensor", None),
        ),
        check_vma=False,
    )
```

```python
import jax
import jax.numpy as jnp
from jax import lax
from jax.experimental import pallas as pl
from jax.experimental.pallas import tpu as pltpu
from jax.sharding import PartitionSpec as P

MESH = pl.DeviceIdType.MESH
SIDE = 8
NEAR_FIRST = (1, 7, 2, 6, 3, 5, 4)


def extend_pages(kv_pages, new_kv, lengths):
    row_count = kv_pages.shape[0]
    step_count = new_kv.shape[1]
    padding = jnp.zeros((row_count, step_count) + kv_pages.shape[2:], kv_pages.dtype)
    grown = jnp.concatenate([kv_pages, padding], axis=1)
    position = jnp.arange(grown.shape[1], dtype=jnp.int32)[None, :]
    for offset in range(step_count):
        hit = (position == lengths[:, None] + offset)[:, :, None, None]
        grown = jnp.where(hit, new_kv[:, offset][:, None], grown)
    return grown


def sending_rows(destination, peer_count):
    row_count = destination.shape[0]
    capacity = (row_count + peer_count - 1) // peer_count
    targets = destination[:, 0]
    row_ids = jnp.arange(row_count, dtype=jnp.int32)
    earlier = row_ids[None, :] < row_ids[:, None]
    same = targets[:, None] == targets[None, :]
    rank = jnp.sum((same & earlier).astype(jnp.int32), axis=1)
    send_slot = targets * capacity + rank
    slot_ids = jnp.arange(peer_count * capacity, dtype=jnp.int32)
    matches = send_slot[None, :] == slot_ids[:, None]
    return jnp.sum(jnp.where(matches, row_ids[None, :], 0), axis=1), jnp.any(matches, axis=1)


def attend(queries, new_kv, kv_cache, lengths):
    rows, steps, _, query_width = queries.shape
    context = kv_cache.shape[1]
    width = kv_cache.shape[3] // 2
    group = query_width // width
    query = queries.reshape(rows, steps * group, width)
    pages = jnp.concatenate([kv_cache[:, :, 0], new_kv[:, :, 0]], axis=1)
    scores = jnp.einsum(
        "nqd,nkd->nqk", query, pages[..., :width], preferred_element_type=jnp.float32
    ) * (width ** (-0.5))
    key_id = jnp.arange(context + steps, dtype=jnp.int32)
    step_id = jnp.arange(steps * group, dtype=jnp.int32) // group
    live = jnp.where(
        (key_id < context)[None, None, :],
        key_id[None, None, :] < lengths[:, None, None],
        (key_id[None, :] - context <= step_id[:, None])[None],
    )
    top = jnp.max(jnp.where(live, scores, -1e30), axis=-1, keepdims=True)
    raised = jnp.where(live, jnp.exp(scores - top), 0.0)
    weights = (raised / jnp.sum(raised, axis=-1, keepdims=True)).astype(jnp.bfloat16)
    summed = jnp.einsum(
        "nqk,nkd->nqd", weights, pages[..., width:], preferred_element_type=jnp.float32
    )
    return summed.astype(jnp.bfloat16).reshape(rows, steps, query_width)


def scan_state(mamba_in, ssm_state, xproj_w, dtproj_w, dt_bias, a_log, d_skip):
    rows, steps, _, width = mamba_in.shape
    low_width = dtproj_w.shape[0]
    state_size = a_log.shape[0]
    x_in = mamba_in[:, :, 0].reshape(rows * steps, width)
    projected = lax.psum(jnp.dot(x_in, xproj_w, preferred_element_type=jnp.float32), "tensor")
    low_rank = projected[:, :low_width].astype(jnp.bfloat16)
    step_size = jax.nn.softplus(
        jnp.dot(low_rank, dtproj_w, preferred_element_type=jnp.float32) + dt_bias
    ).reshape(rows, steps, width)
    b_all = projected[:, low_width : low_width + state_size].reshape(rows, steps, state_size)
    c_all = projected[:, low_width + state_size :].reshape(rows, steps, state_size)
    decay_rate = -jnp.exp(a_log)
    carry = ssm_state
    mixed = []
    for step in range(steps):
        x_float = mamba_in[:, step, 0].astype(jnp.float32)
        z_float = mamba_in[:, step, 1].astype(jnp.float32)
        size = step_size[:, step]
        carry = (
            jnp.exp(size[:, None, :] * decay_rate[None]) * carry
            + b_all[:, step, :, None] * (size * x_float)[:, None, :]
        )
        readout = jnp.sum(carry * c_all[:, step, :, None], axis=1) + d_skip * x_float
        mixed.append((readout * jax.nn.silu(z_float)).astype(jnp.bfloat16))
    return jnp.stack(mixed, axis=1), carry.astype(jnp.bfloat16)


def move_kernel(chosen, rows, out, placed, middle, first_sent, first_come, sent, come):
    me = lax.axis_index("replica")
    shard = lax.axis_index("tensor")
    place = (me // SIDE, me % SIDE)

    def device(route, first, second):
        return (first * SIDE + second if route == 0 else second * SIDE + first, shard)

    barrier = pltpu.get_barrier_semaphore()
    for route in range(2):
        for hop in NEAR_FIRST:
            peer = device(route, lax.rem(place[route] + hop, SIDE), place[1 - route])
            pl.semaphore_signal(barrier, inc=1, device_id=peer, device_id_type=MESH)

    def put(index, carry):
        first, second = index // SIDE, index % SIDE
        placed[0, first, second] = rows[0, chosen[first * SIDE + second]]
        placed[1, first, second] = rows[1, chosen[second * SIDE + first]]
        return carry

    lax.fori_loop(0, SIDE * SIDE, put, 0)
    pl.semaphore_wait(barrier, 2 * len(NEAR_FIRST))

    first_copies = {}
    for hop in NEAR_FIRST:
        for route in range(2):
            target = lax.rem(place[route] + hop, SIDE)
            copy = pltpu.make_async_remote_copy(
                src_ref=placed.at[route, target],
                dst_ref=middle.at[route, hop],
                send_sem=first_sent.at[route, hop],
                recv_sem=first_come.at[route, hop],
                device_id=device(route, target, place[1 - route]),
                device_id_type=MESH,
            )
            copy.start()
            first_copies[route, hop] = copy

    def pass_on(route, bundle, origin):
        mine = place[1 - route]

        def slot(second):
            pair = (origin, second) if route == 0 else (second, origin)
            return out.at[route, pair[0], pair[1]]

        for hop in NEAR_FIRST:
            target = lax.rem(mine + hop, SIDE)
            pltpu.make_async_remote_copy(
                src_ref=bundle.at[target],
                dst_ref=slot(mine),
                send_sem=sent,
                recv_sem=come,
                device_id=device(route, place[route], target),
                device_id_type=MESH,
            ).start()
        slot(mine)[...] = bundle[mine]

    for route in range(2):
        pass_on(route, placed.at[route, place[route]], place[route])
    for hop in NEAR_FIRST:
        for route in range(2):
            first_copies[route, hop].wait_recv()
            origin = lax.rem(place[route] + SIDE - hop, SIDE)
            pass_on(route, middle.at[route, hop], origin)
    for copy in first_copies.values():
        copy.wait_send()
    all_but_own = out.at[:, :, pl.ds(0, SIDE - 1)]
    pltpu.make_async_copy(all_but_own, all_but_own, sent).wait()
    pltpu.make_async_copy(all_but_own, all_but_own, come).wait()


def move_rows(rows, chosen):
    tail = rows.shape[2:]
    whole = (2, SIDE, SIDE) + tail
    moved = pl.pallas_call(
        move_kernel,
        out_shape=jax.ShapeDtypeStruct(whole, rows.dtype),
        in_specs=[
            pl.BlockSpec(memory_space=pltpu.SMEM),
            pl.BlockSpec(memory_space=pltpu.VMEM),
        ],
        out_specs=pl.BlockSpec(memory_space=pltpu.VMEM),
        scratch_shapes=[
            pltpu.VMEM(whole, rows.dtype),
            pltpu.VMEM(whole, rows.dtype),
            pltpu.SemaphoreType.DMA((2, SIDE)),
            pltpu.SemaphoreType.DMA((2, SIDE)),
            pltpu.SemaphoreType.DMA,
            pltpu.SemaphoreType.DMA,
        ],
        name="move_rows",
        compiler_params=pltpu.CompilerParams(
            collective_id=1, has_side_effects=True, vmem_limit_bytes=32 << 20
        ),
    )(chosen, rows)
    return moved.reshape((2, SIDE * SIDE) + tail)


def per_device(
    mamba_in,
    queries,
    new_kv,
    ssm_state,
    kv_cache,
    lengths,
    destination,
    xproj_w,
    dtproj_w,
    dt_bias,
    a_log,
    d_skip,
):
    chosen, present = sending_rows(destination, lax.axis_size("replica"))
    rows, steps, _, width = mamba_in.shape
    state_size = a_log.shape[0]
    query_width = queries.shape[3]
    chosen = jnp.where(present, chosen, rows)
    attended = attend(queries, new_kv, kv_cache, lengths)
    grown = extend_pages(kv_cache, new_kv, lengths)
    mixed, state = scan_state(mamba_in, ssm_state, xproj_w, dtproj_w, dt_bias, a_log, d_skip)
    side = jnp.concatenate(
        [mixed.reshape(rows, -1), attended.reshape(rows, -1), grown.reshape(rows, -1)], axis=1
    )
    side_size = side.shape[1]
    side = side.reshape(rows, state_size, -1)
    cut = width - 128
    half = jnp.concatenate([state[:, :, cut:], side], axis=2)
    half = jnp.pad(half, ((0, 0), (0, 0), (0, cut - half.shape[2])))
    both = jnp.stack([state[:, :, :cut], half])
    both = jnp.pad(both, ((0, 0), (0, 1), (0, 0), (0, 0)))
    main, rest = move_rows(both, chosen)
    slots = main.shape[0]
    out_state = jnp.concatenate([main, rest[:, :, :128]], axis=2)
    rest = rest[:, :, 128 : 128 + side_size // state_size].reshape(slots, side_size)
    mixed_size, attended_size = steps * width, steps * query_width
    return (
        rest[:, :mixed_size].reshape(slots, steps, width),
        rest[:, mixed_size : mixed_size + attended_size].reshape(slots, steps, 1, query_width),
        out_state,
        rest[:, mixed_size + attended_size :].reshape((slots,) + grown.shape[1:]),
    )


def solution(mesh):
    placed = (
        P("replica", None, None, "tensor"),
        P("replica", None, "tensor", None),
        P("replica", None, "tensor", None),
        P("replica", None, "tensor"),
        P("replica", None, "tensor", None),
        P("replica"),
        P("replica", None),
        P("tensor", None),
        P(None, "tensor"),
        P("tensor"),
        P(None, "tensor"),
        P("tensor"),
    )
    return jax.shard_map(
        per_device,
        mesh=mesh,
        in_specs=placed,
        out_specs=(
            P("replica", None, "tensor"),
            P("replica", None, "tensor", None),
            P("replica", None, "tensor"),
            P("replica", None, "tensor", None),
        ),
        check_vma=False,
    )
```

```python
import jax
import jax.numpy as jnp
from jax import lax
from jax.experimental import pallas as pl
from jax.experimental.pallas import tpu as pltpu
from jax.sharding import PartitionSpec as P

MESH = pl.DeviceIdType.MESH
SIDE = 8
NEAR_FIRST = (1, 7, 2, 6, 3, 5, 4)


def sending_rows(destination, peer_count):
    row_count = destination.shape[0]
    capacity = (row_count + peer_count - 1) // peer_count
    targets = destination[:, 0]
    row_ids = jnp.arange(row_count, dtype=jnp.int32)
    earlier = row_ids[None, :] < row_ids[:, None]
    same = targets[:, None] == targets[None, :]
    rank = jnp.sum((same & earlier).astype(jnp.int32), axis=1)
    send_slot = targets * capacity + rank
    slot_ids = jnp.arange(peer_count * capacity, dtype=jnp.int32)
    matches = send_slot[None, :] == slot_ids[:, None]
    return jnp.sum(jnp.where(matches, row_ids[None, :], 0), axis=1), jnp.any(matches, axis=1)


def swap_matrix(first, second):
    size = first * second
    row = lax.broadcasted_iota(jnp.int32, (size, size), 0)
    column = lax.broadcasted_iota(jnp.int32, (size, size), 1)
    return ((row % second) * first + row // second == column).astype(jnp.bfloat16)


def swap_rows(blocks):
    first, second, width = blocks.shape
    swapped = jnp.dot(
        swap_matrix(second, first),
        blocks.reshape(first * second, width),
        preferred_element_type=jnp.float32,
    )
    return swapped.astype(jnp.bfloat16).reshape(second, first, width)


def project_kernel(mamba, weights, total, part, arrived, sum_sent, sum_come, sent, come):
    me = lax.axis_index("tensor")
    peers = lax.axis_size("tensor")
    here = lax.axis_index("replica")
    barrier = pltpu.get_barrier_semaphore()
    for hop in range(1, peers):
        peer = (here, lax.rem(me + hop, peers))
        pl.semaphore_signal(barrier, inc=1, device_id=peer, device_id_type=MESH)
    steps, _, rows, width = mamba.shape
    chunk = part.shape[1]
    per_step = rows // chunk
    for step in range(steps):
        block = lax.dot_general(
            mamba[step, 0],
            weights[...],
            (((1,), (1,)), ((), ())),
            preferred_element_type=jnp.float32,
        )
        for piece in range(per_step):
            part[step * per_step + piece] = block[piece * chunk : (piece + 1) * chunk]
    for piece in range(steps * per_step, peers):
        part[piece] = jnp.zeros(part.shape[1:], part.dtype)
    pl.semaphore_wait(barrier, peers - 1)

    copies = []
    for hop in range(1, peers):
        target = lax.rem(me + hop, peers)
        copy = pltpu.make_async_remote_copy(
            src_ref=part.at[target],
            dst_ref=arrived.at[hop],
            send_sem=sum_sent.at[hop],
            recv_sem=sum_come.at[hop],
            device_id=(here, target),
            device_id_type=MESH,
        )
        copy.start()
        copies.append(copy)
    summed = part[me]
    for hop in range(1, peers):
        copies[hop - 1].wait_recv()
        summed = summed + arrived[hop]
    total[me] = summed
    for hop in range(1, peers):
        target = lax.rem(me + hop, peers)
        copy = pltpu.make_async_remote_copy(
            src_ref=total.at[me],
            dst_ref=total.at[me],
            send_sem=sent.at[hop],
            recv_sem=come.at[hop],
            device_id=(here, target),
            device_id_type=MESH,
        )
        copy.start()
        copies.append(copy)
    for copy in copies[: peers - 1]:
        copy.wait_send()
    for copy in copies[peers - 1 :]:
        copy.wait()


def project(mamba, weights):
    chunk = 8
    peers = lax.axis_size("tensor")
    shape = (peers, chunk, weights.shape[0])
    total = pl.pallas_call(
        project_kernel,
        out_shape=jax.ShapeDtypeStruct(shape, jnp.float32),
        in_specs=[pl.BlockSpec(memory_space=pltpu.VMEM)] * 2,
        out_specs=pl.BlockSpec(memory_space=pltpu.VMEM),
        scratch_shapes=[
            pltpu.VMEM(shape, jnp.float32),
            pltpu.VMEM(shape, jnp.float32),
        ]
        + [pltpu.SemaphoreType.DMA((peers,))] * 4,
        name="project",
        compiler_params=pltpu.CompilerParams(
            collective_id=2, has_side_effects=True, vmem_limit_bytes=32 << 20
        ),
    )(mamba, weights)
    return total.reshape(peers * chunk, weights.shape[0])


def attend(queries, cached, fresh, lengths):
    steps, rows, query_width = queries.shape
    context = cached.shape[1]
    width = cached.shape[2] // 2
    group = query_width // width
    pages = jnp.concatenate(
        [cached.reshape(rows * context, 2 * width), fresh.reshape(steps * rows, 2 * width)], axis=0
    )
    query = jnp.concatenate(
        [queries[s, :, g * width : (g + 1) * width] for s in range(steps) for g in range(group)],
        axis=0,
    )
    scores = lax.dot_general(
        query, pages[:, :width], (((1,), (1,)), ((), ())), preferred_element_type=jnp.float32
    ) * (width ** (-0.5))
    asking = lax.broadcasted_iota(jnp.int32, scores.shape, 0)
    asked = lax.broadcasted_iota(jnp.int32, scores.shape, 1)
    own, step = asking % rows, asking // (group * rows)
    new = asked - rows * context
    cache_live = (new < 0) & (asked // context == own) & (asked % context < lengths)
    fresh_live = (new >= 0) & (new % rows == own) & (new // rows <= step)
    live = cache_live | fresh_live
    top = jnp.max(jnp.where(live, scores, -1e30), axis=-1, keepdims=True)
    raised = jnp.where(live, jnp.exp(scores - top), 0.0)
    weights = (raised / jnp.sum(raised, axis=-1, keepdims=True)).astype(jnp.bfloat16)
    summed = jnp.dot(weights, pages[:, width:], preferred_element_type=jnp.float32)
    summed = summed.astype(jnp.bfloat16)
    return [
        [summed[(s * group + g) * rows : (s * group + g + 1) * rows] for g in range(group)]
        for s in range(steps)
    ]


def grow(cached, fresh, lengths):
    rows, context, width = cached.shape
    steps = fresh.shape[0]
    shape = (rows * context, steps * rows)
    place = lax.broadcasted_iota(jnp.int32, shape, 0)
    token = lax.broadcasted_iota(jnp.int32, shape, 1)
    hit = (place // context == token % rows) & (place % context == lengths + token // rows)
    chosen = jnp.dot(
        hit.astype(jnp.bfloat16),
        fresh.reshape(steps * rows, width),
        preferred_element_type=jnp.float32,
    )
    written = jnp.max(hit.astype(jnp.float32), axis=1, keepdims=True) > 0.0
    kept = cached.reshape(rows * context, width).astype(jnp.float32)
    shape = (steps * rows, steps * rows)
    place = lax.broadcasted_iota(jnp.int32, shape, 0)
    token = lax.broadcasted_iota(jnp.int32, shape, 1)
    hit = (place % rows == token % rows) & (context + place // rows == lengths + token // rows)
    tail = jnp.dot(
        hit.astype(jnp.bfloat16),
        fresh.reshape(steps * rows, width),
        preferred_element_type=jnp.float32,
    )
    grown = jnp.where(written, chosen, kept).astype(jnp.bfloat16)
    return grown.reshape(rows, context, width), tail.astype(jnp.bfloat16).reshape(steps, rows, width)


def decode_kernel(
    mamba,
    queries,
    fresh,
    state,
    cached,
    key_lengths,
    token_lengths,
    total,
    dtproj_w,
    dt_bias,
    a_log,
    d_skip,
    packed,
    decay_rate,
    step_size,
    b_wide,
    c_wide,
    readout,
):
    steps, _, rows, width = mamba.shape
    low_width = dtproj_w.shape[0]
    state_size = a_log.shape[0]
    lane = 128
    page_width = cached.shape[2]
    cut = packed.shape[3] - page_width
    rest = width - cut

    grown, tail = grow(cached[...], fresh[...], token_lengths[...])
    packed[0, :rows, :, cut:] = grown
    attended = attend(queries[...], cached[...], fresh[...], key_lengths[...])
    per_block = page_width // lane
    blocks = [tail[s] for s in range(steps)]
    for step in range(steps):
        for g in range(0, len(attended[step]), per_block):
            blocks.append(jnp.concatenate(attended[step][g : g + per_block], axis=1))
    while len(blocks) < state_size:
        blocks.append(jnp.zeros((rows, page_width), jnp.bfloat16))
    packed[1, :rows, :, cut:] = swap_rows(jnp.stack(blocks))
    packed[0, rows] = jnp.zeros(packed.shape[2:], packed.dtype)
    packed[1, rows] = jnp.zeros(packed.shape[2:], packed.dtype)

    low_rank = total[: steps * rows, :low_width].astype(jnp.bfloat16)
    raw = jnp.dot(low_rank, dtproj_w[...], preferred_element_type=jnp.float32) + dt_bias[...]
    step_size[...] = jnp.maximum(raw, 0.0) + jnp.log1p(jnp.exp(-jnp.abs(raw)))
    decay_rate[...] = -jnp.exp(a_log[...])
    turned = jnp.transpose(total[: steps * rows, low_width:])
    for index in range(steps * rows):
        column = turned[:, index : index + 1]
        b_wide[index] = jnp.broadcast_to(column[:state_size], (state_size, lane))
        c_wide[index] = jnp.broadcast_to(column[state_size:], (state_size, lane))

    for row in range(rows):
        for start in range(0, width, lane):
            span = slice(start, start + lane)
            carry = state[row, :, span]
            for step in range(steps):
                index = step * rows + row
                size = step_size[index : index + 1, span]
                x = mamba[step, 0, row : row + 1, span].astype(jnp.float32)
                carry = jnp.exp(size * decay_rate[:, span]) * carry + b_wide[index] * (size * x)
                readout[index : index + 1, span] = jnp.sum(
                    c_wide[index] * carry, axis=0, keepdims=True
                )
            rounded = carry.astype(jnp.bfloat16)
            if start < cut:
                packed[0, row, :, span] = rounded
            else:
                packed[1, row, :, start - cut : start - cut + lane] = rounded

    blocks = []
    for step in range(steps):
        x = mamba[step, 0].astype(jnp.float32)
        z = mamba[step, 1].astype(jnp.float32)
        whole = readout[step * rows : (step + 1) * rows] + d_skip[...] * x
        mixed = (whole * (z / (1.0 + jnp.exp(-z)))).astype(jnp.bfloat16)
        for start in range(0, width, page_width):
            blocks.append(mixed[:, start : start + page_width])
    while len(blocks) < state_size:
        blocks.append(jnp.zeros((rows, page_width), jnp.bfloat16))
    packed[1, :rows, :, rest:cut] = swap_rows(jnp.stack(blocks))


def decode(mamba, queries, fresh, state, cached, lengths, total, dtproj_w, dt_bias, a_log, d_skip):
    steps, _, rows, width = mamba.shape
    context = cached.shape[1]
    page_width = cached.shape[2]
    state_size = a_log.shape[0]
    key_lengths = jnp.concatenate([jnp.repeat(lengths, context), jnp.tile(lengths, steps)])
    token_lengths = jnp.tile(lengths, steps)
    half = (width + 3 * page_width) // 2
    operands = (
        mamba,
        queries,
        fresh,
        state,
        cached,
        key_lengths[None],
        token_lengths[None],
        total,
        dtproj_w,
        dt_bias[None],
        a_log,
        d_skip[None],
    )
    return pl.pallas_call(
        decode_kernel,
        out_shape=jax.ShapeDtypeStruct((2, rows + 1, state_size, half), jnp.bfloat16),
        in_specs=[pl.BlockSpec(memory_space=pltpu.VMEM)] * len(operands),
        out_specs=pl.BlockSpec(memory_space=pltpu.VMEM),
        scratch_shapes=[
            pltpu.VMEM((state_size, width), jnp.float32),
            pltpu.VMEM((steps * rows, width), jnp.float32),
            pltpu.VMEM((steps * rows, state_size, 128), jnp.float32),
            pltpu.VMEM((steps * rows, state_size, 128), jnp.float32),
            pltpu.VMEM((steps * rows, width), jnp.float32),
        ],
        name="decode",
        compiler_params=pltpu.CompilerParams(vmem_limit_bytes=32 << 20),
    )(*operands)


def unpack_kernel(main, rest, mixed, attended, state, pages):
    steps, _, width = mixed.shape
    page_width = pages.shape[2]
    cut = main.shape[3] - page_width
    left = width - cut
    context = main.shape[2]
    state[:, :, :cut] = main[0, :, :, :cut]
    state[:, :, cut:] = rest[0, :, :, :left]
    pages[:context] = swap_rows(main[0, :, :, cut:])
    swapped = swap_rows(rest[0, :, :, cut:])
    pages[context:] = swapped[:steps]
    per_step = width // page_width
    for step in range(steps):
        for piece in range(per_step):
            span = slice(piece * page_width, (piece + 1) * page_width)
            attended[step, :, span] = swapped[steps + step * per_step + piece]
    swapped = swap_rows(rest[0, :, :, left:cut])
    for step in range(steps):
        for piece in range(per_step):
            span = slice(piece * page_width, (piece + 1) * page_width)
            mixed[step, :, span] = swapped[step * per_step + piece]


def unpack(moved, steps, width, page_width):
    _, slots, state_size, half = moved.shape
    block = 16
    return pl.pallas_call(
        unpack_kernel,
        grid=(slots // block,),
        out_shape=(
            jax.ShapeDtypeStruct((steps, slots, width), jnp.bfloat16),
            jax.ShapeDtypeStruct((steps, slots, width), jnp.bfloat16),
            jax.ShapeDtypeStruct((slots, state_size, width), jnp.bfloat16),
            jax.ShapeDtypeStruct((state_size + steps, slots, page_width), jnp.bfloat16),
        ),
        in_specs=[
            pl.BlockSpec((1, block, state_size, half), lambda i: (0, i, 0, 0)),
            pl.BlockSpec((1, block, state_size, half), lambda i: (1, i, 0, 0)),
        ],
        out_specs=(
            pl.BlockSpec((steps, block, width), lambda i: (0, i, 0)),
            pl.BlockSpec((steps, block, width), lambda i: (0, i, 0)),
            pl.BlockSpec((block, state_size, width), lambda i: (i, 0, 0)),
            pl.BlockSpec((state_size + steps, block, page_width), lambda i: (0, i, 0)),
        ),
        name="unpack",
        compiler_params=pltpu.CompilerParams(vmem_limit_bytes=32 << 20),
    )(moved, moved)


def move_kernel(chosen, rows, out, placed, middle, first_sent, first_come, sent, come):
    me = lax.axis_index("replica")
    shard = lax.axis_index("tensor")
    place = (me // SIDE, me % SIDE)

    def device(route, first, second):
        return (first * SIDE + second if route == 0 else second * SIDE + first, shard)

    barrier = pltpu.get_barrier_semaphore()
    for route in range(2):
        for hop in NEAR_FIRST:
            peer = device(route, lax.rem(place[route] + hop, SIDE), place[1 - route])
            pl.semaphore_signal(barrier, inc=1, device_id=peer, device_id_type=MESH)

    def put(index, carry):
        first, second = index // SIDE, index % SIDE
        placed[0, first, second] = rows[0, chosen[first * SIDE + second]]
        placed[1, first, second] = rows[1, chosen[second * SIDE + first]]
        return carry

    lax.fori_loop(0, SIDE * SIDE, put, 0)
    pl.semaphore_wait(barrier, 2 * len(NEAR_FIRST))

    first_copies = {}
    for hop in NEAR_FIRST:
        for route in range(2):
            target = lax.rem(place[route] + hop, SIDE)
            copy = pltpu.make_async_remote_copy(
                src_ref=placed.at[route, target],
                dst_ref=middle.at[route, hop],
                send_sem=first_sent.at[route, hop],
                recv_sem=first_come.at[route, hop],
                device_id=device(route, target, place[1 - route]),
                device_id_type=MESH,
            )
            copy.start()
            first_copies[route, hop] = copy

    def pass_on(route, bundle, origin):
        mine = place[1 - route]

        def slot(second):
            pair = (origin, second) if route == 0 else (second, origin)
            return out.at[route, pair[0], pair[1]]

        for hop in NEAR_FIRST:
            target = lax.rem(mine + hop, SIDE)
            pltpu.make_async_remote_copy(
                src_ref=bundle.at[target],
                dst_ref=slot(mine),
                send_sem=sent,
                recv_sem=come,
                device_id=device(route, place[route], target),
                device_id_type=MESH,
            ).start()
        slot(mine)[...] = bundle[mine]

    for route in range(2):
        pass_on(route, placed.at[route, place[route]], place[route])
    for hop in NEAR_FIRST:
        for route in range(2):
            first_copies[route, hop].wait_recv()
            origin = lax.rem(place[route] + SIDE - hop, SIDE)
            pass_on(route, middle.at[route, hop], origin)
    for copy in first_copies.values():
        copy.wait_send()
    all_but_own = out.at[:, :, pl.ds(0, SIDE - 1)]
    pltpu.make_async_copy(all_but_own, all_but_own, sent).wait()
    pltpu.make_async_copy(all_but_own, all_but_own, come).wait()


def move_rows(rows, chosen):
    tail = rows.shape[2:]
    whole = (2, SIDE, SIDE) + tail
    moved = pl.pallas_call(
        move_kernel,
        out_shape=jax.ShapeDtypeStruct(whole, rows.dtype),
        in_specs=[
            pl.BlockSpec(memory_space=pltpu.SMEM),
            pl.BlockSpec(memory_space=pltpu.VMEM),
        ],
        out_specs=pl.BlockSpec(memory_space=pltpu.VMEM),
        scratch_shapes=[
            pltpu.VMEM(whole, rows.dtype),
            pltpu.VMEM(whole, rows.dtype),
            pltpu.SemaphoreType.DMA((2, SIDE)),
            pltpu.SemaphoreType.DMA((2, SIDE)),
            pltpu.SemaphoreType.DMA,
            pltpu.SemaphoreType.DMA,
        ],
        name="move_rows",
        compiler_params=pltpu.CompilerParams(
            collective_id=1, has_side_effects=True, vmem_limit_bytes=32 << 20
        ),
    )(chosen, rows)
    return moved.reshape((2, SIDE * SIDE) + tail)


def per_device(
    mamba_in,
    queries,
    new_kv,
    ssm_state,
    kv_cache,
    lengths,
    destination,
    xproj_w,
    dtproj_w,
    dt_bias,
    a_log,
    d_skip,
):
    chosen, present = sending_rows(destination, lax.axis_size("replica"))
    rows, steps, _, width = mamba_in.shape
    chosen = jnp.where(present, chosen, rows)
    mamba = jnp.transpose(mamba_in, (1, 2, 0, 3))
    total = project(mamba, xproj_w.T)
    packed = decode(
        mamba,
        jnp.transpose(queries[:, :, 0], (1, 0, 2)),
        jnp.transpose(new_kv[:, :, 0], (1, 0, 2)),
        ssm_state,
        kv_cache[:, :, 0],
        lengths,
        total,
        dtproj_w,
        dt_bias,
        a_log,
        d_skip,
    )
    moved = move_rows(packed, chosen)
    mixed, attended, state, pages = unpack(moved, steps, width, kv_cache.shape[3])
    return (
        jnp.transpose(mixed, (1, 0, 2)),
        jnp.transpose(attended, (1, 0, 2))[:, :, None],
        state,
        jnp.transpose(pages, (1, 0, 2))[:, :, None],
    )


def solution(mesh):
    placed = (
        P("replica", None, None, "tensor"),
        P("replica", None, "tensor", None),
        P("replica", None, "tensor", None),
        P("replica", None, "tensor"),
        P("replica", None, "tensor", None),
        P("replica"),
        P("replica", None),
        P("tensor", None),
        P(None, "tensor"),
        P("tensor"),
        P(None, "tensor"),
        P("tensor"),
    )
    return jax.shard_map(
        per_device,
        mesh=mesh,
        in_specs=placed,
        out_specs=(
            P("replica", None, "tensor"),
            P("replica", None, "tensor", None),
            P("replica", None, "tensor"),
            P("replica", None, "tensor", None),
        ),
        check_vma=False,
    )
```

```python
import jax
import jax.numpy as jnp
from jax import lax
from jax.experimental import pallas as pl
from jax.experimental.pallas import tpu as pltpu
from jax.sharding import PartitionSpec as P

MESH = pl.DeviceIdType.MESH
SIDE = 8
NEAR_FIRST = (1, 7, 2, 6, 3, 5, 4)


def swap_matrix(first, second):
    size = first * second
    row = lax.broadcasted_iota(jnp.int32, (size, size), 0)
    column = lax.broadcasted_iota(jnp.int32, (size, size), 1)
    return ((row % second) * first + row // second == column).astype(jnp.bfloat16)


def swap_rows(blocks):
    first, second, width = blocks.shape
    swapped = jnp.dot(
        swap_matrix(second, first),
        blocks.reshape(first * second, width),
        preferred_element_type=jnp.float32,
    )
    return swapped.astype(jnp.bfloat16).reshape(second, first, width)


def attend(queries, cached, fresh, lengths):
    steps, rows, query_width = queries.shape
    context = cached.shape[1]
    width = cached.shape[2] // 2
    group = query_width // width
    pages = jnp.concatenate(
        [cached.reshape(rows * context, 2 * width), fresh.reshape(steps * rows, 2 * width)], axis=0
    )
    query = jnp.concatenate(
        [queries[s, :, g * width : (g + 1) * width] for s in range(steps) for g in range(group)],
        axis=0,
    )
    scores = lax.dot_general(
        query, pages[:, :width], (((1,), (1,)), ((), ())), preferred_element_type=jnp.float32
    ) * (width ** (-0.5))
    asking = lax.broadcasted_iota(jnp.int32, scores.shape, 0)
    asked = lax.broadcasted_iota(jnp.int32, scores.shape, 1)
    own, step = asking % rows, asking // (group * rows)
    new = asked - rows * context
    cache_live = (new < 0) & (asked // context == own) & (asked % context < lengths)
    fresh_live = (new >= 0) & (new % rows == own) & (new // rows <= step)
    live = cache_live | fresh_live
    top = jnp.max(jnp.where(live, scores, -1e30), axis=-1, keepdims=True)
    raised = jnp.where(live, jnp.exp(scores - top), 0.0)
    weights = (raised / jnp.sum(raised, axis=-1, keepdims=True)).astype(jnp.bfloat16)
    summed = jnp.dot(weights, pages[:, width:], preferred_element_type=jnp.float32)
    summed = summed.astype(jnp.bfloat16)
    return [
        [summed[(s * group + g) * rows : (s * group + g + 1) * rows] for g in range(group)]
        for s in range(steps)
    ]


def grow(cached, fresh, lengths):
    rows, context, width = cached.shape
    steps = fresh.shape[0]
    shape = (rows * context, steps * rows)
    place = lax.broadcasted_iota(jnp.int32, shape, 0)
    token = lax.broadcasted_iota(jnp.int32, shape, 1)
    hit = (place // context == token % rows) & (place % context == lengths + token // rows)
    chosen = jnp.dot(
        hit.astype(jnp.bfloat16),
        fresh.reshape(steps * rows, width),
        preferred_element_type=jnp.float32,
    )
    written = jnp.max(hit.astype(jnp.float32), axis=1, keepdims=True) > 0.0
    kept = cached.reshape(rows * context, width).astype(jnp.float32)
    shape = (steps * rows, steps * rows)
    place = lax.broadcasted_iota(jnp.int32, shape, 0)
    token = lax.broadcasted_iota(jnp.int32, shape, 1)
    hit = (place % rows == token % rows) & (context + place // rows == lengths + token // rows)
    tail = jnp.dot(
        hit.astype(jnp.bfloat16),
        fresh.reshape(steps * rows, width),
        preferred_element_type=jnp.float32,
    )
    grown = jnp.where(written, chosen, kept).astype(jnp.bfloat16)
    return grown.reshape(rows, context, width), tail.astype(jnp.bfloat16).reshape(steps, rows, width)


def attention_kernel(
    lengths, destination, queries_in, fresh_in, cached_in, packed, chosen, queries, fresh, cached, come
):
    copies = [
        pltpu.make_async_copy(source, held, come.at[index])
        for index, (source, held) in enumerate(
            [(queries_in, queries), (fresh_in, fresh), (cached_in, cached)]
        )
    ]
    for copy in copies:
        copy.start()
    rows, context, page_width = cached.shape
    steps = queries.shape[0]
    state_size = packed.shape[2]

    def clear(slot, carry):
        chosen[slot] = rows
        return carry

    def choose(row, carry):
        chosen[destination[row]] = row
        return carry

    lax.fori_loop(0, chosen.shape[0], clear, 0)
    lax.fori_loop(0, rows, choose, 0)

    token = lax.broadcasted_iota(jnp.int32, (1, steps * rows), 1)
    asked = lax.broadcasted_iota(jnp.int32, (1, rows * context + steps * rows), 1)
    key_row = jnp.where(asked < rows * context, asked // context, (asked - rows * context) % rows)
    key_lengths = jnp.zeros_like(asked)
    token_lengths = jnp.zeros_like(token)
    for row in range(rows):
        key_lengths = jnp.where(key_row == row, lengths[row], key_lengths)
        token_lengths = jnp.where(token % rows == row, lengths[row], token_lengths)
    for copy in copies:
        copy.wait()
    grown, tail = grow(cached[...], fresh[...], token_lengths)
    packed[0, :rows] = grown
    attended = attend(queries[...], cached[...], fresh[...], key_lengths)
    per_block = page_width // 128
    blocks = [tail[s] for s in range(steps)]
    for step in range(steps):
        for g in range(0, len(attended[step]), per_block):
            blocks.append(jnp.concatenate(attended[step][g : g + per_block], axis=1))
    while len(blocks) < state_size:
        blocks.append(jnp.zeros((rows, page_width), jnp.bfloat16))
    packed[1, :rows] = swap_rows(jnp.stack(blocks))
    packed[0, rows] = jnp.zeros(packed.shape[2:], packed.dtype)
    packed[1, rows] = jnp.zeros(packed.shape[2:], packed.dtype)


def attention(queries, fresh, cached, lengths, destination, slots, state_size):
    rows, _, page_width = cached.shape
    arrays = (queries, fresh, cached)
    return pl.pallas_call(
        attention_kernel,
        out_shape=(
            jax.ShapeDtypeStruct((2, rows + 1, state_size, page_width), jnp.bfloat16),
            jax.ShapeDtypeStruct((slots,), jnp.int32),
        ),
        in_specs=[pl.BlockSpec(memory_space=pltpu.SMEM)] * 2
        + [pl.BlockSpec(memory_space=pl.ANY)] * 3,
        out_specs=(
            pl.BlockSpec(memory_space=pltpu.VMEM),
            pl.BlockSpec(memory_space=pltpu.SMEM),
        ),
        scratch_shapes=[pltpu.VMEM(array.shape, array.dtype) for array in arrays]
        + [pltpu.SemaphoreType.DMA((3,))],
        name="attention",
        compiler_params=pltpu.CompilerParams(vmem_limit_bytes=32 << 20),
    )(lengths, destination, *arrays)


def move_kernel(
    chosen,
    early,
    mamba_in,
    xproj_in,
    dtproj_in,
    bias_in,
    a_log_in,
    skip_in,
    state_in,
    out_early,
    out_late,
    mamba,
    xproj,
    dtproj,
    bias,
    a_log,
    skip,
    state,
    part,
    arrived,
    total,
    decay_rate,
    step_size,
    drive,
    b_wide,
    c_wide,
    readout,
    moved_state,
    late_mixed,
    placed_early,
    placed_late,
    middle_early,
    middle_late,
    loaded,
    sum_sent,
    sum_come,
    total_sent,
    total_come,
    first_sent,
    first_come,
    sent,
    come,
    kept,
):
    me = lax.axis_index("replica")
    shard = lax.axis_index("tensor")
    shards = lax.axis_size("tensor")
    place = (me // SIDE, me % SIDE)

    def device(route, first, second):
        return (first * SIDE + second if route == 0 else second * SIDE + first, shard)

    barrier = pltpu.get_barrier_semaphore()
    for hop in range(1, shards):
        peer = (me, lax.rem(shard + hop, shards))
        pl.semaphore_signal(barrier, inc=1, device_id=peer, device_id_type=MESH)
    for route in range(2):
        for hop in NEAR_FIRST:
            peer = device(route, lax.rem(place[route] + hop, SIDE), place[1 - route])
            pl.semaphore_signal(barrier, inc=1, device_id=peer, device_id_type=MESH)

    loads = [
        pltpu.make_async_copy(source, held, loaded.at[index])
        for index, (source, held) in enumerate(
            [
                (mamba_in, mamba),
                (xproj_in, xproj),
                (dtproj_in, dtproj),
                (bias_in, bias),
                (a_log_in, a_log),
                (skip_in, skip),
                (state_in, state),
            ]
        )
    ]
    for load in loads:
        load.start()

    def put_early(index, unused):
        first, second = index // SIDE, index % SIDE
        placed_early[0, first, second] = early[0, chosen[first * SIDE + second]]
        placed_early[1, first, second] = early[1, chosen[second * SIDE + first]]
        return unused

    stages = ((placed_early, middle_early, out_early), (placed_late, middle_late, out_late))
    first_copies = {}

    def send_first(stage):
        placed, middle, _ = stages[stage]
        for hop in NEAR_FIRST:
            for route in range(2):
                target = lax.rem(place[route] + hop, SIDE)
                copy = pltpu.make_async_remote_copy(
                    src_ref=placed.at[route, target],
                    dst_ref=middle.at[route, hop],
                    send_sem=first_sent.at[stage, route, hop],
                    recv_sem=first_come.at[stage, route, hop],
                    device_id=device(route, target, place[1 - route]),
                    device_id_type=MESH,
                )
                copy.start()
                first_copies[stage, route, hop] = copy

    def pass_on(stage, route, bundle, origin):
        mine = place[1 - route]
        out = stages[stage][2]
        pair = (origin, mine) if route == 0 else (mine, origin)
        slot = out.at[route, pair[0], pair[1]]
        for hop in NEAR_FIRST:
            target = lax.rem(mine + hop, SIDE)
            pltpu.make_async_remote_copy(
                src_ref=bundle.at[target],
                dst_ref=slot,
                send_sem=sent.at[stage],
                recv_sem=come.at[stage],
                device_id=device(route, place[route], target),
                device_id_type=MESH,
            ).start()
        pltpu.make_async_copy(bundle.at[mine], slot, kept.at[stage]).start()

    def pass_own(stage):
        for route in range(2):
            pass_on(stage, route, stages[stage][0].at[route, place[route]], place[route])

    def pass_arrived(stage):
        for hop in NEAR_FIRST:
            for route in range(2):
                first_copies[stage, route, hop].wait_recv()
                origin = lax.rem(place[route] + SIDE - hop, SIDE)
                pass_on(stage, route, stages[stage][1].at[route, hop], origin)

    lax.fori_loop(0, SIDE * SIDE, put_early, 0)
    loads[0].wait()
    loads[1].wait()
    steps, _, rows, width = mamba.shape
    chunk = part.shape[1]
    per_step = rows // chunk
    for step in range(steps):
        block = lax.dot_general(
            mamba[step, 0],
            xproj[...],
            (((1,), (1,)), ((), ())),
            preferred_element_type=jnp.float32,
        )
        for piece in range(per_step):
            part[step * per_step + piece] = block[piece * chunk : (piece + 1) * chunk]
    for piece in range(steps * per_step, shards):
        part[piece] = jnp.zeros(part.shape[1:], part.dtype)
    pl.semaphore_wait(barrier, shards - 1 + 2 * len(NEAR_FIRST))

    sums = []
    for hop in range(1, shards):
        target = lax.rem(shard + hop, shards)
        copy = pltpu.make_async_remote_copy(
            src_ref=part.at[target],
            dst_ref=arrived.at[hop],
            send_sem=sum_sent.at[hop],
            recv_sem=sum_come.at[hop],
            device_id=(me, target),
            device_id_type=MESH,
        )
        copy.start()
        sums.append(copy)
    send_first(0)
    pass_own(0)
    for load in loads[2:]:
        load.wait()
    decay_rate[...] = -jnp.exp(a_log[...])
    moved_state[rows] = jnp.zeros(moved_state.shape[1:], moved_state.dtype)
    late_mixed[rows] = jnp.zeros(late_mixed.shape[1:], late_mixed.dtype)

    summed = part[shard]
    for hop in range(1, shards):
        sums[hop - 1].wait_recv()
        summed = summed + arrived[hop]
    total[shard] = summed
    totals = []
    for hop in range(1, shards):
        target = lax.rem(shard + hop, shards)
        copy = pltpu.make_async_remote_copy(
            src_ref=total.at[shard],
            dst_ref=total.at[shard],
            send_sem=total_sent.at[hop],
            recv_sem=total_come.at[hop],
            device_id=(me, target),
            device_id_type=MESH,
        )
        copy.start()
        totals.append(copy)
    for copy in totals:
        copy.wait_recv()

    low_width = dtproj.shape[0]
    state_size = a_log.shape[0]
    lane = 128
    projected = total[...].reshape(shards * chunk, total.shape[2])[: steps * rows]
    low_rank = projected[:, :low_width].astype(jnp.bfloat16)
    raw = jnp.dot(low_rank, dtproj[...], preferred_element_type=jnp.float32) + bias[...]
    step_size[...] = jnp.maximum(raw, 0.0) + jnp.log1p(jnp.exp(-jnp.abs(raw)))
    for step in range(steps):
        span = slice(step * rows, (step + 1) * rows)
        drive[span] = step_size[span] * mamba[step, 0].astype(jnp.float32)
    turned = jnp.transpose(projected[:, low_width:])
    for index in range(steps * rows):
        column = turned[:, index : index + 1]
        b_wide[index] = jnp.broadcast_to(column[:state_size], (state_size, lane))
        c_wide[index] = jnp.broadcast_to(column[state_size:], (state_size, lane))

    cut = placed_late.shape[4]
    rest = width - cut

    def update(piece, unused):
        span = pl.ds(pl.multiple_of(piece * lane, lane), lane)
        rate = decay_rate[:, span]
        for row in range(rows):
            carry = state[row, :, span]
            for step in range(steps):
                index = step * rows + row
                size = step_size[index : index + 1, span]
                carry = (
                    jnp.exp(size * rate) * carry
                    + b_wide[index] * drive[index : index + 1, span]
                )
                readout[index : index + 1, span] = jnp.sum(
                    c_wide[index] * carry, axis=0, keepdims=True
                )
            moved_state[row, :, span] = carry.astype(jnp.bfloat16)
        return unused

    lax.fori_loop(0, width // lane, update, 0)
    page_width = cut - rest
    blocks = []
    for step in range(steps):
        x = mamba[step, 0].astype(jnp.float32)
        z = mamba[step, 1].astype(jnp.float32)
        whole = readout[step * rows : (step + 1) * rows] + skip[...] * x
        mixed = (whole * (z / (1.0 + jnp.exp(-z)))).astype(jnp.bfloat16)
        for start in range(0, width, page_width):
            blocks.append(mixed[:, start : start + page_width])
    while len(blocks) < state_size:
        blocks.append(jnp.zeros((rows, page_width), jnp.bfloat16))
    late_mixed[:rows] = swap_rows(jnp.stack(blocks))

    def put_late(index, unused):
        first, second = index // SIDE, index % SIDE
        placed_late[0, first, second] = moved_state[chosen[first * SIDE + second], :, :cut]
        row = chosen[second * SIDE + first]
        placed_late[1, first, second, :, :rest] = moved_state[row, :, cut:]
        placed_late[1, first, second, :, rest:] = late_mixed[row]
        return unused

    lax.fori_loop(0, SIDE * SIDE, put_late, 0)
    send_first(1)
    pass_own(1)
    pass_arrived(0)
    pass_arrived(1)
    for copy in sums + totals + list(first_copies.values()):
        copy.wait_send()
    for stage in range(2):
        out = stages[stage][2]
        others = out.at[:, :, pl.ds(0, SIDE - 1)]
        own = out.at[:, :, 0]
        pltpu.make_async_copy(own, own, kept.at[stage]).wait()
        pltpu.make_async_copy(others, others, sent.at[stage]).wait()
        pltpu.make_async_copy(others, others, come.at[stage]).wait()


def move_rows(chosen, early, mamba, xproj_w, dtproj_w, dt_bias, a_log, d_skip, state):
    steps, _, rows, width = mamba.shape
    state_size = a_log.shape[0]
    page_width = early.shape[3]
    half = (width + page_width) // 2
    shards = lax.axis_size("tensor")
    arrays = (mamba, xproj_w, dtproj_w, dt_bias, a_log, d_skip, state)
    grid = (2, SIDE, SIDE, state_size)
    early_grid, late_grid = grid + (page_width,), grid + (half,)
    sums = (shards, steps * rows // 6, xproj_w.shape[0])
    outs = pl.pallas_call(
        move_kernel,
        out_shape=(
            jax.ShapeDtypeStruct(early_grid, jnp.bfloat16),
            jax.ShapeDtypeStruct(late_grid, jnp.bfloat16),
        ),
        in_specs=[
            pl.BlockSpec(memory_space=pltpu.SMEM),
            pl.BlockSpec(memory_space=pltpu.VMEM),
        ]
        + [pl.BlockSpec(memory_space=pl.ANY)] * len(arrays),
        out_specs=(pl.BlockSpec(memory_space=pl.ANY), pl.BlockSpec(memory_space=pl.ANY)),
        scratch_shapes=[pltpu.VMEM(array.shape, array.dtype) for array in arrays]
        + [pltpu.VMEM(sums, jnp.float32)] * 3
        + [
            pltpu.VMEM((state_size, width), jnp.float32),
            pltpu.VMEM((steps * rows, width), jnp.float32),
            pltpu.VMEM((steps * rows, width), jnp.float32),
            pltpu.VMEM((steps * rows, state_size, 128), jnp.float32),
            pltpu.VMEM((steps * rows, state_size, 128), jnp.float32),
            pltpu.VMEM((steps * rows, width), jnp.float32),
            pltpu.VMEM((rows + 1, state_size, width), jnp.bfloat16),
            pltpu.VMEM((rows + 1, state_size, page_width), jnp.bfloat16),
            pltpu.VMEM(early_grid, jnp.bfloat16),
            pltpu.VMEM(late_grid, jnp.bfloat16),
            pltpu.VMEM(early_grid, jnp.bfloat16),
            pltpu.VMEM(late_grid, jnp.bfloat16),
            pltpu.SemaphoreType.DMA((len(arrays),)),
        ]
        + [pltpu.SemaphoreType.DMA((shards,))] * 4
        + [pltpu.SemaphoreType.DMA((2, 2, SIDE))] * 2
        + [pltpu.SemaphoreType.DMA((2,))] * 3,
        name="move_rows",
        compiler_params=pltpu.CompilerParams(
            collective_id=1, has_side_effects=True, vmem_limit_bytes=32 << 20
        ),
    )(chosen, early, *arrays)
    return [out.reshape((2, SIDE * SIDE) + out.shape[3:]) for out in outs]


def unpack_kernel(early, late, mixed, attended, state, pages):
    steps, _, width = mixed.shape
    page_width = pages.shape[2]
    cut = late.shape[3]
    left = width - cut
    context = early.shape[2]
    state[:, :, :cut] = late[0]
    state[:, :, cut:] = late[1, :, :, :left]
    pages[:context] = swap_rows(early[0])
    swapped = swap_rows(early[1])
    pages[context:] = swapped[:steps]
    per_step = width // page_width
    for step in range(steps):
        for piece in range(per_step):
            span = slice(piece * page_width, (piece + 1) * page_width)
            attended[step, :, span] = swapped[steps + step * per_step + piece]
    swapped = swap_rows(late[1, :, :, left:])
    for step in range(steps):
        for piece in range(per_step):
            span = slice(piece * page_width, (piece + 1) * page_width)
            mixed[step, :, span] = swapped[step * per_step + piece]


def unpack(early, late, steps, width):
    _, slots, state_size, page_width = early.shape
    half = late.shape[3]
    block = 16
    return pl.pallas_call(
        unpack_kernel,
        grid=(slots // block,),
        out_shape=(
            jax.ShapeDtypeStruct((steps, slots, width), jnp.bfloat16),
            jax.ShapeDtypeStruct((steps, slots, width), jnp.bfloat16),
            jax.ShapeDtypeStruct((slots, state_size, width), jnp.bfloat16),
            jax.ShapeDtypeStruct((state_size + steps, slots, page_width), jnp.bfloat16),
        ),
        in_specs=[
            pl.BlockSpec((2, block, state_size, page_width), lambda i: (0, i, 0, 0)),
            pl.BlockSpec((2, block, state_size, half), lambda i: (0, i, 0, 0)),
        ],
        out_specs=(
            pl.BlockSpec((steps, block, width), lambda i: (0, i, 0)),
            pl.BlockSpec((steps, block, width), lambda i: (0, i, 0)),
            pl.BlockSpec((block, state_size, width), lambda i: (i, 0, 0)),
            pl.BlockSpec((state_size + steps, block, page_width), lambda i: (0, i, 0)),
        ),
        name="unpack",
        compiler_params=pltpu.CompilerParams(vmem_limit_bytes=32 << 20),
    )(early, late)


def per_device(
    mamba_in,
    queries,
    new_kv,
    ssm_state,
    kv_cache,
    lengths,
    destination,
    xproj_w,
    dtproj_w,
    dt_bias,
    a_log,
    d_skip,
):
    steps, width = mamba_in.shape[1], mamba_in.shape[3]
    early, chosen = attention(
        jnp.transpose(queries[:, :, 0], (1, 0, 2)),
        jnp.transpose(new_kv[:, :, 0], (1, 0, 2)),
        kv_cache[:, :, 0],
        lengths,
        destination[:, 0],
        lax.axis_size("replica"),
        a_log.shape[0],
    )
    early, late = move_rows(
        chosen,
        early,
        jnp.transpose(mamba_in, (1, 2, 0, 3)),
        xproj_w.T,
        dtproj_w,
        dt_bias[None],
        a_log,
        d_skip[None],
        ssm_state,
    )
    mixed, attended, state, pages = unpack(early, late, steps, width)
    return (
        jnp.transpose(mixed, (1, 0, 2)),
        jnp.transpose(attended, (1, 0, 2))[:, :, None],
        state,
        jnp.transpose(pages, (1, 0, 2))[:, :, None],
    )


def solution(mesh):
    placed = (
        P("replica", None, None, "tensor"),
        P("replica", None, "tensor", None),
        P("replica", None, "tensor", None),
        P("replica", None, "tensor"),
        P("replica", None, "tensor", None),
        P("replica"),
        P("replica", None),
        P("tensor", None),
        P(None, "tensor"),
        P("tensor"),
        P(None, "tensor"),
        P("tensor"),
    )
    return jax.shard_map(
        per_device,
        mesh=mesh,
        in_specs=placed,
        out_specs=(
            P("replica", None, "tensor"),
            P("replica", None, "tensor", None),
            P("replica", None, "tensor"),
            P("replica", None, "tensor", None),
        ),
        check_vma=False,
    )
```

```python
import jax
import jax.numpy as jnp
from jax import lax
from jax.experimental import pallas as pl
from jax.experimental.pallas import tpu as pltpu
from jax.sharding import PartitionSpec as P

MESH = pl.DeviceIdType.MESH
SIDE = 8
NEAR_FIRST = (1, 7, 2, 6, 3, 5, 4)
BLOCK_HOPS = (1, 2, 3, -1, -2)


def swap_matrix(first, second):
    size = first * second
    row = lax.broadcasted_iota(jnp.int32, (size, size), 0)
    column = lax.broadcasted_iota(jnp.int32, (size, size), 1)
    return ((row % second) * first + row // second == column).astype(jnp.bfloat16)


def swap_rows(blocks):
    first, second, width = blocks.shape
    swapped = jnp.dot(
        swap_matrix(second, first),
        blocks.reshape(first * second, width),
        preferred_element_type=jnp.float32,
    )
    return swapped.astype(jnp.bfloat16).reshape(second, first, width)


def attend(queries, cached, fresh, lengths):
    steps, rows, query_width = queries.shape
    context = cached.shape[1]
    width = cached.shape[2] // 2
    group = query_width // width
    pages = jnp.concatenate(
        [cached.reshape(rows * context, 2 * width), fresh.reshape(steps * rows, 2 * width)], axis=0
    )
    query = jnp.concatenate(
        [queries[s, :, g * width : (g + 1) * width] for s in range(steps) for g in range(group)],
        axis=0,
    )
    scores = lax.dot_general(
        query, pages[:, :width], (((1,), (1,)), ((), ())), preferred_element_type=jnp.float32
    ) * (width ** (-0.5))
    asking = lax.broadcasted_iota(jnp.int32, scores.shape, 0)
    asked = lax.broadcasted_iota(jnp.int32, scores.shape, 1)
    own, step = asking % rows, asking // (group * rows)
    new = asked - rows * context
    cache_live = (new < 0) & (asked // context == own) & (asked % context < lengths)
    fresh_live = (new >= 0) & (new % rows == own) & (new // rows <= step)
    live = cache_live | fresh_live
    top = jnp.max(jnp.where(live, scores, -1e30), axis=-1, keepdims=True)
    raised = jnp.where(live, jnp.exp(scores - top), 0.0)
    weights = (raised / jnp.sum(raised, axis=-1, keepdims=True)).astype(jnp.bfloat16)
    summed = jnp.dot(weights, pages[:, width:], preferred_element_type=jnp.float32)
    summed = summed.astype(jnp.bfloat16)
    return [
        [summed[(s * group + g) * rows : (s * group + g + 1) * rows] for g in range(group)]
        for s in range(steps)
    ]


def grow(cached, fresh, lengths):
    rows, context, width = cached.shape
    steps = fresh.shape[0]
    shape = (rows * context, steps * rows)
    place = lax.broadcasted_iota(jnp.int32, shape, 0)
    token = lax.broadcasted_iota(jnp.int32, shape, 1)
    hit = (place // context == token % rows) & (place % context == lengths + token // rows)
    chosen = jnp.dot(
        hit.astype(jnp.bfloat16),
        fresh.reshape(steps * rows, width),
        preferred_element_type=jnp.float32,
    )
    written = jnp.max(hit.astype(jnp.float32), axis=1, keepdims=True) > 0.0
    kept = cached.reshape(rows * context, width).astype(jnp.float32)
    shape = (steps * rows, steps * rows)
    place = lax.broadcasted_iota(jnp.int32, shape, 0)
    token = lax.broadcasted_iota(jnp.int32, shape, 1)
    hit = (place % rows == token % rows) & (context + place // rows == lengths + token // rows)
    tail = jnp.dot(
        hit.astype(jnp.bfloat16),
        fresh.reshape(steps * rows, width),
        preferred_element_type=jnp.float32,
    )
    grown = jnp.where(written, chosen, kept).astype(jnp.bfloat16)
    return grown.reshape(rows, context, width), tail.astype(jnp.bfloat16).reshape(steps, rows, width)


def attention_kernel(
    lengths, destination, queries_in, fresh_in, cached_in, packed, chosen, queries, fresh, cached, come
):
    copies = [
        pltpu.make_async_copy(source, held, come.at[index])
        for index, (source, held) in enumerate(
            [(queries_in, queries), (fresh_in, fresh), (cached_in, cached)]
        )
    ]
    for copy in copies:
        copy.start()
    rows, context, page_width = cached.shape
    steps = queries.shape[0]
    state_size = packed.shape[2]

    def clear(slot, carry):
        chosen[slot] = rows
        return carry

    def choose(row, carry):
        chosen[destination[row]] = row
        return carry

    lax.fori_loop(0, chosen.shape[0], clear, 0)
    lax.fori_loop(0, rows, choose, 0)

    token = lax.broadcasted_iota(jnp.int32, (1, steps * rows), 1)
    asked = lax.broadcasted_iota(jnp.int32, (1, rows * context + steps * rows), 1)
    key_row = jnp.where(asked < rows * context, asked // context, (asked - rows * context) % rows)
    key_lengths = jnp.zeros_like(asked)
    token_lengths = jnp.zeros_like(token)
    for row in range(rows):
        key_lengths = jnp.where(key_row == row, lengths[row], key_lengths)
        token_lengths = jnp.where(token % rows == row, lengths[row], token_lengths)
    for copy in copies:
        copy.wait()
    grown, tail = grow(cached[...], fresh[...], token_lengths)
    packed[0, :rows] = grown
    attended = attend(queries[...], cached[...], fresh[...], key_lengths)
    per_block = page_width // 128
    blocks = [tail[s] for s in range(steps)]
    for step in range(steps):
        for g in range(0, len(attended[step]), per_block):
            blocks.append(jnp.concatenate(attended[step][g : g + per_block], axis=1))
    while len(blocks) < state_size:
        blocks.append(jnp.zeros((rows, page_width), jnp.bfloat16))
    packed[1, :rows] = swap_rows(jnp.stack(blocks))
    packed[0, rows] = jnp.zeros(packed.shape[2:], packed.dtype)
    packed[1, rows] = jnp.zeros(packed.shape[2:], packed.dtype)


def attention(queries, fresh, cached, lengths, destination, slots, state_size):
    rows, _, page_width = cached.shape
    arrays = (queries, fresh, cached)
    return pl.pallas_call(
        attention_kernel,
        out_shape=(
            jax.ShapeDtypeStruct((2, rows + 1, state_size, page_width), jnp.bfloat16),
            jax.ShapeDtypeStruct((slots,), jnp.int32),
        ),
        in_specs=[pl.BlockSpec(memory_space=pltpu.SMEM)] * 2
        + [pl.BlockSpec(memory_space=pl.ANY)] * 3,
        out_specs=(
            pl.BlockSpec(memory_space=pltpu.VMEM),
            pl.BlockSpec(memory_space=pltpu.SMEM),
        ),
        scratch_shapes=[pltpu.VMEM(array.shape, array.dtype) for array in arrays]
        + [pltpu.SemaphoreType.DMA((3,))],
        name="attention",
        compiler_params=pltpu.CompilerParams(vmem_limit_bytes=60 << 20),
    )(lengths, destination, *arrays)


def move_kernel(
    chosen,
    table,
    early,
    mamba_in,
    xproj_in,
    dtproj_in,
    bias_in,
    a_log_in,
    skip_in,
    state_in,
    out_early,
    out_late,
    mamba,
    xproj,
    dtproj,
    bias,
    a_log,
    skip,
    state,
    part,
    arrived,
    total,
    decay_rate,
    step_size,
    drive,
    b_wide,
    c_wide,
    readout,
    late,
    bundles_early,
    bundles_late,
    tables_come,
    tables,
    loaded,
    sum_sent,
    sum_come,
    total_sent,
    total_come,
    table_sent,
    table_come,
    table_kept,
    first_sent,
    first_come,
    sent,
    come,
    kept,
    *blocks,
):
    me = lax.axis_index("replica")
    shard = lax.axis_index("tensor")
    shards = lax.axis_size("tensor")
    place = (me // SIDE, me % SIDE)
    ahead = 1 - 2 * lax.rem(shard, 2)

    def device(route, first, second):
        return (first * SIDE + second if route == 0 else second * SIDE + first, shard)

    def along(route, hop):
        return lax.rem(place[route] + hop * ahead + SIDE, SIDE)

    barrier = pltpu.get_barrier_semaphore()
    for hop in range(1, shards):
        peer = (me, lax.rem(shard + hop, shards))
        pl.semaphore_signal(barrier, inc=1, device_id=peer, device_id_type=MESH)
    for route in range(2):
        for hop in NEAR_FIRST:
            peer = device(route, lax.rem(place[route] + hop, SIDE), place[1 - route])
            pl.semaphore_signal(barrier, inc=1, device_id=peer, device_id_type=MESH)

    loads = [
        pltpu.make_async_copy(source, held, loaded.at[index])
        for index, (source, held) in enumerate(
            [
                (mamba_in, mamba),
                (xproj_in, xproj),
                (dtproj_in, dtproj),
                (bias_in, bias),
                (a_log_in, a_log),
                (skip_in, skip),
                (state_in, state),
            ]
        )
    ]
    for load in loads:
        load.start()

    steps, _, rows, width = mamba.shape
    sources = (early, late)
    bundles = (bundles_early, bundles_late)
    outs = (out_early, out_late)
    hops = len(BLOCK_HOPS)

    def block_of(stage, route, which):
        return blocks[(stage * 2 + route) * hops + which]

    for stage in range(2):
        for route in range(2):
            for which in range(hops):
                block = block_of(stage, route, which)
                block[rows] = jnp.zeros(block.shape[1:], block.dtype)
    for route in range(2):
        late[route, rows] = jnp.zeros(late.shape[2:], late.dtype)

    started = []

    def ship(source, target, stage, route, which, step):
        copy = pltpu.make_async_remote_copy(
            src_ref=source,
            dst_ref=target,
            send_sem=first_sent.at[stage, route, which],
            recv_sem=first_come.at[stage, route, which],
            device_id=device(route, along(route, step), place[1 - route]),
            device_id_type=MESH,
        )
        copy.start()
        started.append(copy)
        return copy

    def select(stage, route, block, slots, first, kind):
        def one(second, unused):
            slot = first * SIDE + second if route == 0 else second * SIDE + first
            bundles[stage][route, kind, second] = block[slots(slot)]
            return unused

        lax.fori_loop(0, SIDE, one, 0)

    def pass_on(stage, route, kind, hop):
        mine = place[1 - route]
        origin = along(route, -hop)
        pair = (origin, mine) if route == 0 else (mine, origin)
        slot = outs[stage].at[route, pair[0], pair[1]]
        for step in NEAR_FIRST:
            target = lax.rem(mine + step, SIDE)
            pltpu.make_async_remote_copy(
                src_ref=bundles[stage].at[route, kind, target],
                dst_ref=slot,
                send_sem=sent.at[stage],
                recv_sem=come.at[stage],
                device_id=device(route, place[route], target),
                device_id_type=MESH,
            ).start()
        pltpu.make_async_copy(
            bundles[stage].at[route, kind, mine], slot, kept.at[stage]
        ).start()

    def pass_own(stage):
        for route in range(2):
            block = sources[stage].at[route]
            select(stage, route, block, lambda slot: chosen[slot], place[route], 0)
            pass_on(stage, route, 0, 0)

    def pass_block(stage, route, which):
        select(
            stage,
            route,
            block_of(stage, route, which),
            lambda slot: tables[route, which, 0, slot],
            place[route],
            1 + which,
        )
        pass_on(stage, route, 1 + which, BLOCK_HOPS[which])

    legs = {}

    def start_block(stage, route, which, source, step):
        target = block_of(stage, route, which).at[pl.ds(0, rows)]
        legs[stage, route, which] = ship(
            source.at[pl.ds(0, rows)], target, stage, route, which, step
        )

    def start_bundle(stage, route, which, kind, step):
        select(
            stage,
            route,
            block_of(stage, route, which),
            lambda slot: tables[route, which, 0, slot],
            along(route, step),
            kind,
        )
        held = bundles[stage]
        legs[stage, route, kind] = ship(
            held.at[route, kind], held.at[route, kind + 2], stage, route, kind, step
        )

    def first_leg(stage):
        for route in range(2):
            start_block(stage, route, 0, sources[stage].at[route], 1)
            start_block(stage, route, 3, sources[stage].at[route], -1)

    def second_leg(stage):
        for route in range(2):
            legs[stage, route, 0].wait_recv()
            start_block(stage, route, 1, block_of(stage, route, 0), 1)
            legs[stage, route, 3].wait_recv()
            start_block(stage, route, 4, block_of(stage, route, 3), -1)
        for route in range(2):
            pass_block(stage, route, 0)
            pass_block(stage, route, 3)

    def third_leg(stage):
        for route in range(2):
            legs[stage, route, 1].wait_recv()
            start_block(stage, route, 2, block_of(stage, route, 1), 1)
            legs[stage, route, 4].wait_recv()
            start_bundle(stage, route, 4, 6, -1)
        for route in range(2):
            pass_block(stage, route, 1)
            pass_block(stage, route, 4)

    def fourth_leg(stage):
        for route in range(2):
            legs[stage, route, 2].wait_recv()
            start_bundle(stage, route, 2, 7, 1)
        for route in range(2):
            pass_block(stage, route, 2)
            legs[stage, route, 6].wait_recv()
            pass_on(stage, route, 8, -3)

    def last_leg(stage):
        for route in range(2):
            legs[stage, route, 7].wait_recv()
            pass_on(stage, route, 9, 4)

    pl.semaphore_wait(barrier, shards - 1 + 2 * len(NEAR_FIRST))
    table_legs = []
    for which, hop in enumerate(BLOCK_HOPS):
        for route in range(2):
            copy = pltpu.make_async_remote_copy(
                src_ref=table,
                dst_ref=tables_come.at[route, which],
                send_sem=table_sent.at[route, which],
                recv_sem=table_come.at[route, which],
                device_id=device(route, along(route, hop), place[1 - route]),
                device_id_type=MESH,
            )
            copy.start()
            table_legs.append(copy)
    first_leg(0)
    pass_own(0)

    loads[0].wait()
    loads[1].wait()
    chunk = part.shape[1]
    per_step = rows // chunk
    for step in range(steps):
        block = lax.dot_general(
            mamba[step, 0],
            xproj[...],
            (((1,), (1,)), ((), ())),
            preferred_element_type=jnp.float32,
        )
        for piece in range(per_step):
            part[step * per_step + piece] = block[piece * chunk : (piece + 1) * chunk]
    for piece in range(steps * per_step, shards):
        part[piece] = jnp.zeros(part.shape[1:], part.dtype)
    sums = []
    for hop in range(1, shards):
        target = lax.rem(shard + hop, shards)
        copy = pltpu.make_async_remote_copy(
            src_ref=part.at[target],
            dst_ref=arrived.at[hop],
            send_sem=sum_sent.at[hop],
            recv_sem=sum_come.at[hop],
            device_id=(me, target),
            device_id_type=MESH,
        )
        copy.start()
        sums.append(copy)
    for copy in table_legs:
        copy.wait_recv()
    keep = pltpu.make_async_copy(tables_come, tables, table_kept)
    keep.start()
    keep.wait()
    for load in loads[2:]:
        load.wait()
    decay_rate[...] = -jnp.exp(a_log[...])

    summed = part[shard]
    for hop in range(1, shards):
        sums[hop - 1].wait_recv()
        summed = summed + arrived[hop]
    total[shard] = summed
    totals = []
    for hop in range(1, shards):
        target = lax.rem(shard + hop, shards)
        copy = pltpu.make_async_remote_copy(
            src_ref=total.at[shard],
            dst_ref=total.at[shard],
            send_sem=total_sent.at[hop],
            recv_sem=total_come.at[hop],
            device_id=(me, target),
            device_id_type=MESH,
        )
        copy.start()
        totals.append(copy)
    second_leg(0)
    for copy in totals:
        copy.wait_recv()

    low_width = dtproj.shape[0]
    state_size = a_log.shape[0]
    lane = 128
    projected = total[...].reshape(shards * chunk, total.shape[2])[: steps * rows]
    low_rank = projected[:, :low_width].astype(jnp.bfloat16)
    raw = jnp.dot(low_rank, dtproj[...], preferred_element_type=jnp.float32) + bias[...]
    step_size[...] = jnp.maximum(raw, 0.0) + jnp.log1p(jnp.exp(-jnp.abs(raw)))
    for step in range(steps):
        span = slice(step * rows, (step + 1) * rows)
        drive[span] = step_size[span] * mamba[step, 0].astype(jnp.float32)
    turned = jnp.transpose(projected[:, low_width:])
    for index in range(steps * rows):
        column = turned[:, index : index + 1]
        b_wide[index] = jnp.broadcast_to(column[:state_size], (state_size, lane))
        c_wide[index] = jnp.broadcast_to(column[state_size:], (state_size, lane))

    cut = late.shape[3]
    rest = width - cut

    def update(route, skipped):
        def one(piece, unused):
            span = pl.ds(pl.multiple_of(piece * lane + skipped, lane), lane)
            goal = pl.ds(pl.multiple_of(piece * lane, lane), lane)
            rate = decay_rate[:, span]
            for row in range(rows):
                carry = state[row, :, span]
                for step in range(steps):
                    index = step * rows + row
                    size = step_size[index : index + 1, span]
                    carry = (
                        jnp.exp(size * rate) * carry
                        + b_wide[index] * drive[index : index + 1, span]
                    )
                    readout[index : index + 1, span] = jnp.sum(
                        c_wide[index] * carry, axis=0, keepdims=True
                    )
                late[route, row, :, goal] = carry.astype(jnp.bfloat16)
            return unused

        return one

    lax.fori_loop(0, cut // lane, update(0, 0), 0)
    lax.fori_loop(0, rest // lane, update(1, cut), 0)
    page_width = cut - rest
    pieces = []
    for step in range(steps):
        x = mamba[step, 0].astype(jnp.float32)
        z = mamba[step, 1].astype(jnp.float32)
        whole = readout[step * rows : (step + 1) * rows] + skip[...] * x
        mixed = (whole * (z / (1.0 + jnp.exp(-z)))).astype(jnp.bfloat16)
        for start in range(0, width, page_width):
            pieces.append(mixed[:, start : start + page_width])
    while len(pieces) < state_size:
        pieces.append(jnp.zeros((rows, page_width), jnp.bfloat16))
    late[1, :rows, :, rest:] = swap_rows(jnp.stack(pieces))

    first_leg(1)
    third_leg(0)
    pass_own(1)
    fourth_leg(0)
    second_leg(1)
    last_leg(0)
    third_leg(1)
    fourth_leg(1)
    last_leg(1)

    for copy in table_legs + sums + totals + started:
        copy.wait_send()
    for stage in range(2):
        others = outs[stage].at[:, :, pl.ds(0, SIDE - 1)]
        own = outs[stage].at[:, :, 0]
        pltpu.make_async_copy(own, own, kept.at[stage]).wait()
        pltpu.make_async_copy(others, others, sent.at[stage]).wait()
        pltpu.make_async_copy(others, others, come.at[stage]).wait()


def move_rows(chosen, early, mamba, xproj_w, dtproj_w, dt_bias, a_log, d_skip, state):
    steps, _, rows, width = mamba.shape
    state_size = a_log.shape[0]
    page_width = early.shape[3]
    half = (width + page_width) // 2
    shards = lax.axis_size("tensor")
    arrays = (mamba, xproj_w, dtproj_w, dt_bias, a_log, d_skip, state)
    grid = (2, SIDE, SIDE, state_size)
    kinds = (2, 10, SIDE, state_size)
    early_grid, late_grid = grid + (page_width,), grid + (half,)
    sums = (shards, steps * rows // 6, xproj_w.shape[0])
    tables = (2, len(BLOCK_HOPS), 1, chosen.shape[0])
    early_block = pltpu.VMEM((rows + 1, state_size, page_width), jnp.bfloat16)
    late_block = pltpu.VMEM((rows + 1, state_size, half), jnp.bfloat16)
    blocks = [early_block] * (2 * len(BLOCK_HOPS)) + [late_block] * (2 * len(BLOCK_HOPS))
    outs = pl.pallas_call(
        move_kernel,
        out_shape=(
            jax.ShapeDtypeStruct(early_grid, jnp.bfloat16),
            jax.ShapeDtypeStruct(late_grid, jnp.bfloat16),
        ),
        in_specs=[
            pl.BlockSpec(memory_space=pltpu.SMEM),
            pl.BlockSpec(memory_space=pltpu.VMEM),
            pl.BlockSpec(memory_space=pltpu.VMEM),
        ]
        + [pl.BlockSpec(memory_space=pl.ANY)] * len(arrays),
        out_specs=(pl.BlockSpec(memory_space=pl.ANY), pl.BlockSpec(memory_space=pl.ANY)),
        scratch_shapes=[pltpu.VMEM(array.shape, array.dtype) for array in arrays]
        + [pltpu.VMEM(sums, jnp.float32)] * 3
        + [
            pltpu.VMEM((state_size, width), jnp.float32),
            pltpu.VMEM((steps * rows, width), jnp.float32),
            pltpu.VMEM((steps * rows, width), jnp.float32),
            pltpu.VMEM((steps * rows, state_size, 128), jnp.float32),
            pltpu.VMEM((steps * rows, state_size, 128), jnp.float32),
            pltpu.VMEM((steps * rows, width), jnp.float32),
            pltpu.VMEM((2, rows + 1, state_size, half), jnp.bfloat16),
            pltpu.VMEM(kinds + (page_width,), jnp.bfloat16),
            pltpu.VMEM(kinds + (half,), jnp.bfloat16),
            pltpu.VMEM(tables, jnp.int32),
            pltpu.SMEM(tables, jnp.int32),
            pltpu.SemaphoreType.DMA((len(arrays),)),
        ]
        + [pltpu.SemaphoreType.DMA((shards,))] * 4
        + [pltpu.SemaphoreType.DMA((2, len(BLOCK_HOPS)))] * 2
        + [pltpu.SemaphoreType.DMA]
        + [pltpu.SemaphoreType.DMA((2, 2, SIDE))] * 2
        + [pltpu.SemaphoreType.DMA((2,))] * 3
        + blocks,
        name="move_rows",
        compiler_params=pltpu.CompilerParams(
            collective_id=1, has_side_effects=True, vmem_limit_bytes=60 << 20
        ),
    )(chosen, chosen[None], early, *arrays)
    return [out.reshape((2, SIDE * SIDE) + out.shape[3:]) for out in outs]


def unpack_kernel(early, late, mixed, attended, state, pages):
    steps, _, width = mixed.shape
    page_width = pages.shape[2]
    cut = late.shape[3]
    left = width - cut
    context = early.shape[2]
    state[:, :, :cut] = late[0]
    state[:, :, cut:] = late[1, :, :, :left]
    pages[:context] = swap_rows(early[0])
    swapped = swap_rows(early[1])
    pages[context:] = swapped[:steps]
    per_step = width // page_width
    for step in range(steps):
        for piece in range(per_step):
            span = slice(piece * page_width, (piece + 1) * page_width)
            attended[step, :, span] = swapped[steps + step * per_step + piece]
    swapped = swap_rows(late[1, :, :, left:])
    for step in range(steps):
        for piece in range(per_step):
            span = slice(piece * page_width, (piece + 1) * page_width)
            mixed[step, :, span] = swapped[step * per_step + piece]


def unpack(early, late, steps, width):
    _, slots, state_size, page_width = early.shape
    half = late.shape[3]
    block = 16
    return pl.pallas_call(
        unpack_kernel,
        grid=(slots // block,),
        out_shape=(
            jax.ShapeDtypeStruct((steps, slots, width), jnp.bfloat16),
            jax.ShapeDtypeStruct((steps, slots, width), jnp.bfloat16),
            jax.ShapeDtypeStruct((slots, state_size, width), jnp.bfloat16),
            jax.ShapeDtypeStruct((state_size + steps, slots, page_width), jnp.bfloat16),
        ),
        in_specs=[
            pl.BlockSpec((2, block, state_size, page_width), lambda i: (0, i, 0, 0)),
            pl.BlockSpec((2, block, state_size, half), lambda i: (0, i, 0, 0)),
        ],
        out_specs=(
            pl.BlockSpec((steps, block, width), lambda i: (0, i, 0)),
            pl.BlockSpec((steps, block, width), lambda i: (0, i, 0)),
            pl.BlockSpec((block, state_size, width), lambda i: (i, 0, 0)),
            pl.BlockSpec((state_size + steps, block, page_width), lambda i: (0, i, 0)),
        ),
        name="unpack",
        compiler_params=pltpu.CompilerParams(vmem_limit_bytes=60 << 20),
    )(early, late)


def per_device(
    mamba_in,
    queries,
    new_kv,
    ssm_state,
    kv_cache,
    lengths,
    destination,
    xproj_w,
    dtproj_w,
    dt_bias,
    a_log,
    d_skip,
):
    steps, width = mamba_in.shape[1], mamba_in.shape[3]
    early, chosen = attention(
        jnp.transpose(queries[:, :, 0], (1, 0, 2)),
        jnp.transpose(new_kv[:, :, 0], (1, 0, 2)),
        kv_cache[:, :, 0],
        lengths,
        destination[:, 0],
        2 * lax.axis_size("replica"),
        a_log.shape[0],
    )
    early, late = move_rows(
        chosen,
        early,
        jnp.transpose(mamba_in, (1, 2, 0, 3)),
        xproj_w.T,
        dtproj_w,
        dt_bias[None],
        a_log,
        d_skip[None],
        ssm_state,
    )
    mixed, attended, state, pages = unpack(early, late, steps, width)
    return (
        jnp.transpose(mixed, (1, 0, 2)),
        jnp.transpose(attended, (1, 0, 2))[:, :, None],
        state,
        jnp.transpose(pages, (1, 0, 2))[:, :, None],
    )


def solution(mesh):
    placed = (
        P("replica", None, None, "tensor"),
        P("replica", None, "tensor", None),
        P("replica", None, "tensor", None),
        P("replica", None, "tensor"),
        P("replica", None, "tensor", None),
        P("replica"),
        P("replica", None),
        P("tensor", None),
        P(None, "tensor"),
        P("tensor"),
        P(None, "tensor"),
        P("tensor"),
    )
    return jax.shard_map(
        per_device,
        mesh=mesh,
        in_specs=placed,
        out_specs=(
            P("replica", None, "tensor"),
            P("replica", None, "tensor", None),
            P("replica", None, "tensor"),
            P("replica", None, "tensor", None),
        ),
        check_vma=False,
    )
```

```python
import jax
import jax.numpy as jnp
from jax import lax
from jax.experimental import pallas as pl
from jax.experimental.pallas import tpu as pltpu
from jax.sharding import PartitionSpec as P

MESH = pl.DeviceIdType.MESH
SIDE = 8
NEAR_FIRST = (1, 7, 2, 6, 3, 5, 4)
BLOCK_HOPS = (1, 2, 3, -1, -2)


def swap_matrix(first, second):
    size = first * second
    row = lax.broadcasted_iota(jnp.int32, (size, size), 0)
    column = lax.broadcasted_iota(jnp.int32, (size, size), 1)
    return ((row % second) * first + row // second == column).astype(jnp.bfloat16)


def swap_rows(blocks):
    first, second, width = blocks.shape
    swapped = jnp.dot(
        swap_matrix(second, first),
        blocks.reshape(first * second, width),
        preferred_element_type=jnp.float32,
    )
    return swapped.astype(jnp.bfloat16).reshape(second, first, width)


def attend(queries, cached, fresh, lengths):
    steps, rows, query_width = queries.shape
    context = cached.shape[1]
    width = cached.shape[2] // 2
    group = query_width // width
    pages = jnp.concatenate(
        [cached.reshape(rows * context, 2 * width), fresh.reshape(steps * rows, 2 * width)], axis=0
    )
    query = jnp.concatenate(
        [queries[s, :, g * width : (g + 1) * width] for s in range(steps) for g in range(group)],
        axis=0,
    )
    scores = lax.dot_general(
        query, pages[:, :width], (((1,), (1,)), ((), ())), preferred_element_type=jnp.float32
    ) * (width ** (-0.5))
    asking = lax.broadcasted_iota(jnp.int32, scores.shape, 0)
    asked = lax.broadcasted_iota(jnp.int32, scores.shape, 1)
    own, step = asking % rows, asking // (group * rows)
    new = asked - rows * context
    cache_live = (new < 0) & (asked // context == own) & (asked % context < lengths)
    fresh_live = (new >= 0) & (new % rows == own) & (new // rows <= step)
    live = cache_live | fresh_live
    top = jnp.max(jnp.where(live, scores, -1e30), axis=-1, keepdims=True)
    raised = jnp.where(live, jnp.exp(scores - top), 0.0)
    weights = (raised / jnp.sum(raised, axis=-1, keepdims=True)).astype(jnp.bfloat16)
    summed = jnp.dot(weights, pages[:, width:], preferred_element_type=jnp.float32)
    summed = summed.astype(jnp.bfloat16)
    return [
        [summed[(s * group + g) * rows : (s * group + g + 1) * rows] for g in range(group)]
        for s in range(steps)
    ]


def grow(cached, fresh, lengths):
    rows, context, width = cached.shape
    steps = fresh.shape[0]
    shape = (rows * context, steps * rows)
    place = lax.broadcasted_iota(jnp.int32, shape, 0)
    token = lax.broadcasted_iota(jnp.int32, shape, 1)
    hit = (place // context == token % rows) & (place % context == lengths + token // rows)
    chosen = jnp.dot(
        hit.astype(jnp.bfloat16),
        fresh.reshape(steps * rows, width),
        preferred_element_type=jnp.float32,
    )
    written = jnp.max(hit.astype(jnp.float32), axis=1, keepdims=True) > 0.0
    kept = cached.reshape(rows * context, width).astype(jnp.float32)
    shape = (steps * rows, steps * rows)
    place = lax.broadcasted_iota(jnp.int32, shape, 0)
    token = lax.broadcasted_iota(jnp.int32, shape, 1)
    hit = (place % rows == token % rows) & (context + place // rows == lengths + token // rows)
    tail = jnp.dot(
        hit.astype(jnp.bfloat16),
        fresh.reshape(steps * rows, width),
        preferred_element_type=jnp.float32,
    )
    grown = jnp.where(written, chosen, kept).astype(jnp.bfloat16)
    return grown.reshape(rows, context, width), tail.astype(jnp.bfloat16).reshape(steps, rows, width)


def move_kernel(
    lengths,
    destination,
    mamba_in,
    xproj_in,
    cached_in,
    fresh_in,
    queries_in,
    dtproj_in,
    bias_in,
    a_log_in,
    skip_in,
    state_in,
    out_early,
    out_late,
    mamba,
    xproj,
    cached,
    fresh,
    queries,
    dtproj,
    bias,
    a_log,
    skip,
    state,
    part,
    arrived,
    total,
    decay_rate,
    step_size,
    drive,
    b_wide,
    c_wide,
    readout,
    early,
    late,
    bundles_early,
    bundles_late,
    table,
    chosen,
    tables_come,
    tables,
    loaded,
    sum_sent,
    sum_come,
    total_sent,
    total_come,
    table_sent,
    table_come,
    table_kept,
    first_sent,
    first_come,
    sent,
    come,
    kept,
    *blocks,
):
    me = lax.axis_index("replica")
    shard = lax.axis_index("tensor")
    shards = lax.axis_size("tensor")
    place = (me // SIDE, me % SIDE)
    ahead = 1 - 2 * lax.rem(shard, 2)

    def device(route, first, second):
        return (first * SIDE + second if route == 0 else second * SIDE + first, shard)

    def along(route, hop):
        return lax.rem(place[route] + hop * ahead + SIDE, SIDE)

    barrier = pltpu.get_barrier_semaphore()
    for hop in range(1, shards):
        peer = (me, lax.rem(shard + hop, shards))
        pl.semaphore_signal(barrier, inc=1, device_id=peer, device_id_type=MESH)
    for route in range(2):
        for hop in NEAR_FIRST:
            peer = device(route, lax.rem(place[route] + hop, SIDE), place[1 - route])
            pl.semaphore_signal(barrier, inc=1, device_id=peer, device_id_type=MESH)

    loads = [
        pltpu.make_async_copy(source, held, loaded.at[index])
        for index, (source, held) in enumerate(
            [
                (mamba_in, mamba),
                (xproj_in, xproj),
                (cached_in, cached),
                (fresh_in, fresh),
                (queries_in, queries),
                (dtproj_in, dtproj),
                (bias_in, bias),
                (a_log_in, a_log),
                (skip_in, skip),
                (state_in, state),
            ]
        )
    ]
    for load in loads:
        load.start()

    steps, _, rows, width = mamba.shape
    sources = (early, late)
    bundles = (bundles_early, bundles_late)
    outs = (out_early, out_late)
    hops = len(BLOCK_HOPS)

    def block_of(stage, route, which):
        return blocks[(stage * 2 + route) * hops + which]

    for stage in range(2):
        for route in range(2):
            for which in range(hops):
                block = block_of(stage, route, which)
                block[rows] = jnp.zeros(block.shape[1:], block.dtype)
    for route in range(2):
        early[route, rows] = jnp.zeros(early.shape[2:], early.dtype)
        late[route, rows] = jnp.zeros(late.shape[2:], late.dtype)
    slot_id = lax.broadcasted_iota(jnp.int32, table.shape, 1)
    slot_row = jnp.full(table.shape, rows, jnp.int32)
    for row in range(rows):
        slot_row = jnp.where(slot_id == destination[row], row, slot_row)
    table[...] = slot_row
    keep_own = pltpu.make_async_copy(table, chosen, table_kept.at[0])
    keep_own.start()

    started = []

    def ship(source, target, stage, route, which, step):
        copy = pltpu.make_async_remote_copy(
            src_ref=source,
            dst_ref=target,
            send_sem=first_sent.at[stage, route, which],
            recv_sem=first_come.at[stage, route, which],
            device_id=device(route, along(route, step), place[1 - route]),
            device_id_type=MESH,
        )
        copy.start()
        started.append(copy)
        return copy

    def select(stage, route, block, slots, first, kind):
        def one(second, unused):
            slot = first * SIDE + second if route == 0 else second * SIDE + first
            bundles[stage][route, kind, second] = block[slots(slot)]
            return unused

        lax.fori_loop(0, SIDE, one, 0)

    def pass_on(stage, route, kind, hop):
        mine = place[1 - route]
        origin = along(route, -hop)
        pair = (origin, mine) if route == 0 else (mine, origin)
        slot = outs[stage].at[route, pair[0], pair[1]]
        for step in NEAR_FIRST:
            target = lax.rem(mine + step, SIDE)
            pltpu.make_async_remote_copy(
                src_ref=bundles[stage].at[route, kind, target],
                dst_ref=slot,
                send_sem=sent.at[stage],
                recv_sem=come.at[stage],
                device_id=device(route, place[route], target),
                device_id_type=MESH,
            ).start()
        pltpu.make_async_copy(
            bundles[stage].at[route, kind, mine], slot, kept.at[stage]
        ).start()

    def pass_own(stage):
        for route in range(2):
            block = sources[stage].at[route]
            select(stage, route, block, lambda slot: chosen[0, slot], place[route], 0)
            pass_on(stage, route, 0, 0)

    def pass_block(stage, route, which):
        select(
            stage,
            route,
            block_of(stage, route, which),
            lambda slot: tables[route, which, 0, slot],
            place[route],
            1 + which,
        )
        pass_on(stage, route, 1 + which, BLOCK_HOPS[which])

    legs = {}

    def start_block(stage, route, which, source, step):
        target = block_of(stage, route, which).at[pl.ds(0, rows)]
        legs[stage, route, which] = ship(
            source.at[pl.ds(0, rows)], target, stage, route, which, step
        )

    def start_bundle(stage, route, which, kind, step):
        select(
            stage,
            route,
            block_of(stage, route, which),
            lambda slot: tables[route, which, 0, slot],
            along(route, step),
            kind,
        )
        held = bundles[stage]
        legs[stage, route, kind] = ship(
            held.at[route, kind], held.at[route, kind + 2], stage, route, kind, step
        )

    def first_leg(stage, route):
        start_block(stage, route, 0, sources[stage].at[route], 1)
        start_block(stage, route, 3, sources[stage].at[route], -1)

    def second_leg(stage):
        for route in range(2):
            legs[stage, route, 0].wait_recv()
            start_block(stage, route, 1, block_of(stage, route, 0), 1)
            legs[stage, route, 3].wait_recv()
            start_block(stage, route, 4, block_of(stage, route, 3), -1)
        for route in range(2):
            pass_block(stage, route, 0)
            pass_block(stage, route, 3)

    def third_leg(stage):
        for route in range(2):
            legs[stage, route, 1].wait_recv()
            start_block(stage, route, 2, block_of(stage, route, 1), 1)
            legs[stage, route, 4].wait_recv()
            start_bundle(stage, route, 4, 6, -1)
        for route in range(2):
            pass_block(stage, route, 1)
            pass_block(stage, route, 4)

    def fourth_leg(stage):
        for route in range(2):
            legs[stage, route, 2].wait_recv()
            start_bundle(stage, route, 2, 7, 1)
        for route in range(2):
            pass_block(stage, route, 2)
            legs[stage, route, 6].wait_recv()
            pass_on(stage, route, 8, -3)

    def last_leg(stage):
        for route in range(2):
            legs[stage, route, 7].wait_recv()
            pass_on(stage, route, 9, 4)

    loads[0].wait()
    loads[1].wait()
    chunk = part.shape[1]
    per_step = rows // chunk
    for step in range(steps):
        block = lax.dot_general(
            mamba[step, 0],
            xproj[...],
            (((1,), (1,)), ((), ())),
            preferred_element_type=jnp.float32,
        )
        for piece in range(per_step):
            part[step * per_step + piece] = block[piece * chunk : (piece + 1) * chunk]
    for piece in range(steps * per_step, shards):
        part[piece] = jnp.zeros(part.shape[1:], part.dtype)
    keep_own.wait()
    pl.semaphore_wait(barrier, shards - 1 + 2 * len(NEAR_FIRST))

    sums = []
    for hop in range(1, shards):
        target = lax.rem(shard + hop, shards)
        copy = pltpu.make_async_remote_copy(
            src_ref=part.at[target],
            dst_ref=arrived.at[hop],
            send_sem=sum_sent.at[hop],
            recv_sem=sum_come.at[hop],
            device_id=(me, target),
            device_id_type=MESH,
        )
        copy.start()
        sums.append(copy)
    table_legs = []
    for which, hop in enumerate(BLOCK_HOPS):
        for route in range(2):
            copy = pltpu.make_async_remote_copy(
                src_ref=table,
                dst_ref=tables_come.at[route, which],
                send_sem=table_sent.at[route, which],
                recv_sem=table_come.at[route, which],
                device_id=device(route, along(route, hop), place[1 - route]),
                device_id_type=MESH,
            )
            copy.start()
            table_legs.append(copy)

    context, page_width = cached.shape[1:]
    token = lax.broadcasted_iota(jnp.int32, (1, steps * rows), 1)
    asked = lax.broadcasted_iota(jnp.int32, (1, rows * context + steps * rows), 1)
    key_row = jnp.where(asked < rows * context, asked // context, (asked - rows * context) % rows)
    key_lengths = jnp.zeros_like(asked)
    token_lengths = jnp.zeros_like(token)
    for row in range(rows):
        key_lengths = jnp.where(key_row == row, lengths[row], key_lengths)
        token_lengths = jnp.where(token % rows == row, lengths[row], token_lengths)
    for load in loads[2:5]:
        load.wait()
    grown, tail = grow(cached[...], fresh[...], token_lengths)
    early[0, :rows] = grown
    first_leg(0, 0)
    attended = attend(queries[...], cached[...], fresh[...], key_lengths)
    per_block = page_width // 128
    pieces = [tail[step] for step in range(steps)]
    for step in range(steps):
        for g in range(0, len(attended[step]), per_block):
            pieces.append(jnp.concatenate(attended[step][g : g + per_block], axis=1))
    while len(pieces) < early.shape[2]:
        pieces.append(jnp.zeros((rows, page_width), jnp.bfloat16))
    early[1, :rows] = swap_rows(jnp.stack(pieces))
    first_leg(0, 1)
    pass_own(0)
    for load in loads[5:]:
        load.wait()
    decay_rate[...] = -jnp.exp(a_log[...])

    summed = part[shard]
    for hop in range(1, shards):
        sums[hop - 1].wait_recv()
        summed = summed + arrived[hop]
    total[shard] = summed
    totals = []
    for hop in range(1, shards):
        target = lax.rem(shard + hop, shards)
        copy = pltpu.make_async_remote_copy(
            src_ref=total.at[shard],
            dst_ref=total.at[shard],
            send_sem=total_sent.at[hop],
            recv_sem=total_come.at[hop],
            device_id=(me, target),
            device_id_type=MESH,
        )
        copy.start()
        totals.append(copy)
    for copy in table_legs:
        copy.wait_recv()
    keep = pltpu.make_async_copy(tables_come, tables, table_kept.at[1])
    keep.start()
    keep.wait()
    second_leg(0)
    for copy in totals:
        copy.wait_recv()

    low_width = dtproj.shape[0]
    state_size = a_log.shape[0]
    lane = 128
    projected = total[...].reshape(shards * chunk, total.shape[2])[: steps * rows]
    low_rank = projected[:, :low_width].astype(jnp.bfloat16)
    raw = jnp.dot(low_rank, dtproj[...], preferred_element_type=jnp.float32) + bias[...]
    step_size[...] = jnp.maximum(raw, 0.0) + jnp.log1p(jnp.exp(-jnp.abs(raw)))
    for step in range(steps):
        span = slice(step * rows, (step + 1) * rows)
        drive[span] = step_size[span] * mamba[step, 0].astype(jnp.float32)
    turned = jnp.transpose(projected[:, low_width:])
    for index in range(steps * rows):
        column = turned[:, index : index + 1]
        b_wide[index] = jnp.broadcast_to(column[:state_size], (state_size, lane))
        c_wide[index] = jnp.broadcast_to(column[state_size:], (state_size, lane))

    cut = late.shape[3]
    rest = width - cut

    def update(route, skipped):
        def one(piece, unused):
            span = pl.ds(pl.multiple_of(piece * lane + skipped, lane), lane)
            goal = pl.ds(pl.multiple_of(piece * lane, lane), lane)
            rate = decay_rate[:, span]
            for row in range(rows):
                carry = state[row, :, span]
                for step in range(steps):
                    index = step * rows + row
                    size = step_size[index : index + 1, span]
                    carry = (
                        jnp.exp(size * rate) * carry
                        + b_wide[index] * drive[index : index + 1, span]
                    )
                    readout[index : index + 1, span] = jnp.sum(
                        c_wide[index] * carry, axis=0, keepdims=True
                    )
                late[route, row, :, goal] = carry.astype(jnp.bfloat16)
            return unused

        return one

    third_leg(0)
    lax.fori_loop(0, cut // lane, update(0, 0), 0)
    first_leg(1, 0)
    lax.fori_loop(0, rest // lane, update(1, cut), 0)
    pieces = []
    for step in range(steps):
        x = mamba[step, 0].astype(jnp.float32)
        z = mamba[step, 1].astype(jnp.float32)
        whole = readout[step * rows : (step + 1) * rows] + skip[...] * x
        mixed = (whole * (z / (1.0 + jnp.exp(-z)))).astype(jnp.bfloat16)
        for start in range(0, width, page_width):
            pieces.append(mixed[:, start : start + page_width])
    while len(pieces) < state_size:
        pieces.append(jnp.zeros((rows, page_width), jnp.bfloat16))
    late[1, :rows, :, rest:] = swap_rows(jnp.stack(pieces))

    first_leg(1, 1)
    pass_own(1)
    fourth_leg(0)
    second_leg(1)
    last_leg(0)
    third_leg(1)
    fourth_leg(1)
    last_leg(1)

    for copy in table_legs + sums + totals + started:
        copy.wait_send()
    for stage in range(2):
        others = outs[stage].at[:, :, pl.ds(0, SIDE - 1)]
        own = outs[stage].at[:, :, 0]
        pltpu.make_async_copy(own, own, kept.at[stage]).wait()
        pltpu.make_async_copy(others, others, sent.at[stage]).wait()
        pltpu.make_async_copy(others, others, come.at[stage]).wait()


def move_rows(lengths, destination, *arrays):
    mamba, xproj_w, cached, a_log = arrays[0], arrays[1], arrays[2], arrays[7]
    steps, _, rows, width = mamba.shape
    state_size = a_log.shape[0]
    page_width = cached.shape[2]
    half = (width + page_width) // 2
    shards = lax.axis_size("tensor")
    grid = (2, SIDE, SIDE, state_size)
    kinds = (2, 10, SIDE, state_size)
    early_grid, late_grid = grid + (page_width,), grid + (half,)
    sums = (shards, steps * rows // 6, xproj_w.shape[0])
    table = (1, 2 * SIDE * SIDE)
    tables = (2, len(BLOCK_HOPS)) + table
    early_block = pltpu.VMEM((rows + 1, state_size, page_width), jnp.bfloat16)
    late_block = pltpu.VMEM((rows + 1, state_size, half), jnp.bfloat16)
    blocks = [early_block] * (2 * len(BLOCK_HOPS)) + [late_block] * (2 * len(BLOCK_HOPS))
    outs = pl.pallas_call(
        move_kernel,
        out_shape=(
            jax.ShapeDtypeStruct(early_grid, jnp.bfloat16),
            jax.ShapeDtypeStruct(late_grid, jnp.bfloat16),
        ),
        in_specs=[
            pl.BlockSpec(memory_space=pltpu.SMEM),
            pl.BlockSpec(memory_space=pltpu.SMEM),
        ]
        + [pl.BlockSpec(memory_space=pl.ANY)] * len(arrays),
        out_specs=(pl.BlockSpec(memory_space=pl.ANY), pl.BlockSpec(memory_space=pl.ANY)),
        scratch_shapes=[pltpu.VMEM(array.shape, array.dtype) for array in arrays]
        + [pltpu.VMEM(sums, jnp.float32)] * 3
        + [
            pltpu.VMEM((state_size, width), jnp.float32),
            pltpu.VMEM((steps * rows, width), jnp.float32),
            pltpu.VMEM((steps * rows, width), jnp.float32),
            pltpu.VMEM((steps * rows, state_size, 128), jnp.float32),
            pltpu.VMEM((steps * rows, state_size, 128), jnp.float32),
            pltpu.VMEM((steps * rows, width), jnp.float32),
            pltpu.VMEM((2, rows + 1, state_size, page_width), jnp.bfloat16),
            pltpu.VMEM((2, rows + 1, state_size, half), jnp.bfloat16),
            pltpu.VMEM(kinds + (page_width,), jnp.bfloat16),
            pltpu.VMEM(kinds + (half,), jnp.bfloat16),
            pltpu.VMEM(table, jnp.int32),
            pltpu.SMEM(table, jnp.int32),
            pltpu.VMEM(tables, jnp.int32),
            pltpu.SMEM(tables, jnp.int32),
            pltpu.SemaphoreType.DMA((len(arrays),)),
        ]
        + [pltpu.SemaphoreType.DMA((shards,))] * 4
        + [pltpu.SemaphoreType.DMA((2, len(BLOCK_HOPS)))] * 2
        + [pltpu.SemaphoreType.DMA((2,))]
        + [pltpu.SemaphoreType.DMA((2, 2, SIDE))] * 2
        + [pltpu.SemaphoreType.DMA((2,))] * 3
        + blocks,
        name="move_rows",
        compiler_params=pltpu.CompilerParams(
            collective_id=1, has_side_effects=True, vmem_limit_bytes=60 << 20
        ),
    )(lengths, destination, *arrays)
    return [out.reshape((2, SIDE * SIDE) + out.shape[3:]) for out in outs]


def unpack_kernel(
    early_in,
    late_in,
    mixed_out,
    attended_out,
    state_out,
    pages_out,
    early,
    late,
    mixed,
    attended,
    pages,
    come,
    gone,
):
    steps, slots, width = mixed.shape
    page_width = pages.shape[2]
    cut = late.shape[3]
    left = width - cut
    context = early.shape[2]
    per_step = width // page_width
    block = 16
    loads = []
    for index in range(slots // block):
        span = pl.ds(index * block, block)
        group = []
        for route in range(2):
            for kind, (source, held) in enumerate([(late_in, late), (early_in, early)]):
                copy = pltpu.make_async_copy(
                    source.at[route, span], held.at[route, span], come.at[index, 2 * route + kind]
                )
                copy.start()
                group.append(copy)
        loads.append(group)
    stores = []

    def store(source, goal, index, which):
        copy = pltpu.make_async_copy(source, goal, gone.at[index, which])
        copy.start()
        stores.append(copy)

    for index, group in enumerate(loads):
        for copy in group:
            copy.wait()
        span = pl.ds(index * block, block)
        rows = slice(index * block, (index + 1) * block)
        store(late.at[0, span], state_out.at[span, :, pl.ds(0, cut)], index, 0)
        store(
            late.at[1, span, :, pl.ds(0, left)], state_out.at[span, :, pl.ds(cut, left)], index, 1
        )
        pages[:context, rows] = swap_rows(early[0, rows])
        swapped = swap_rows(early[1, rows])
        pages[context:, rows] = swapped[:steps]
        store(pages.at[:, span], pages_out.at[:, span], index, 2)
        for step in range(steps):
            for piece in range(per_step):
                lanes = slice(piece * page_width, (piece + 1) * page_width)
                attended[step, rows, lanes] = swapped[steps + step * per_step + piece]
        store(attended.at[:, span], attended_out.at[:, span], index, 3)
        swapped = swap_rows(late[1, rows, :, left:])
        for step in range(steps):
            for piece in range(per_step):
                lanes = slice(piece * page_width, (piece + 1) * page_width)
                mixed[step, rows, lanes] = swapped[step * per_step + piece]
        store(mixed.at[:, span], mixed_out.at[:, span], index, 4)
    for copy in stores:
        copy.wait()


def unpack(early, late, steps, width):
    _, slots, state_size, page_width = early.shape
    wide = (steps, slots, width)
    paged = (state_size + steps, slots, page_width)
    return pl.pallas_call(
        unpack_kernel,
        out_shape=(
            jax.ShapeDtypeStruct(wide, jnp.bfloat16),
            jax.ShapeDtypeStruct(wide, jnp.bfloat16),
            jax.ShapeDtypeStruct((slots, state_size, width), jnp.bfloat16),
            jax.ShapeDtypeStruct(paged, jnp.bfloat16),
        ),
        in_specs=[pl.BlockSpec(memory_space=pl.ANY)] * 2,
        out_specs=(pl.BlockSpec(memory_space=pl.ANY),) * 4,
        scratch_shapes=[
            pltpu.VMEM(early.shape, jnp.bfloat16),
            pltpu.VMEM(late.shape, jnp.bfloat16),
            pltpu.VMEM(wide, jnp.bfloat16),
            pltpu.VMEM(wide, jnp.bfloat16),
            pltpu.VMEM(paged, jnp.bfloat16),
            pltpu.SemaphoreType.DMA((slots // 16, 4)),
            pltpu.SemaphoreType.DMA((slots // 16, 5)),
        ],
        name="unpack",
        compiler_params=pltpu.CompilerParams(vmem_limit_bytes=60 << 20),
    )(early, late)


def per_device(
    mamba_in,
    queries,
    new_kv,
    ssm_state,
    kv_cache,
    lengths,
    destination,
    xproj_w,
    dtproj_w,
    dt_bias,
    a_log,
    d_skip,
):
    steps, width = mamba_in.shape[1], mamba_in.shape[3]
    early, late = move_rows(
        lengths,
        destination[:, 0],
        jnp.transpose(mamba_in, (1, 2, 0, 3)),
        xproj_w.T,
        kv_cache[:, :, 0],
        jnp.transpose(new_kv[:, :, 0], (1, 0, 2)),
        jnp.transpose(queries[:, :, 0], (1, 0, 2)),
        dtproj_w,
        dt_bias[None],
        a_log,
        d_skip[None],
        ssm_state,
    )
    mixed, attended, state, pages = unpack(early, late, steps, width)
    return (
        jnp.transpose(mixed, (1, 0, 2)),
        jnp.transpose(attended, (1, 0, 2))[:, :, None],
        state,
        jnp.transpose(pages, (1, 0, 2))[:, :, None],
    )


def solution(mesh):
    placed = (
        P("replica", None, None, "tensor"),
        P("replica", None, "tensor", None),
        P("replica", None, "tensor", None),
        P("replica", None, "tensor"),
        P("replica", None, "tensor", None),
        P("replica"),
        P("replica", None),
        P("tensor", None),
        P(None, "tensor"),
        P("tensor"),
        P(None, "tensor"),
        P("tensor"),
    )
    return jax.shard_map(
        per_device,
        mesh=mesh,
        in_specs=placed,
        out_specs=(
            P("replica", None, "tensor"),
            P("replica", None, "tensor", None),
            P("replica", None, "tensor"),
            P("replica", None, "tensor", None),
        ),
        check_vma=False,
    )
```

```python
import jax
import jax.numpy as jnp
from jax import lax
from jax.experimental import pallas as pl
from jax.experimental.pallas import tpu as pltpu
from jax.sharding import PartitionSpec as P

MESH = pl.DeviceIdType.MESH
SIDE = 8
NEAR_FIRST = (1, 7, 2, 6, 3, 5, 4)
BLOCK_HOPS = (1, 2, 3, -1, -2)


def swap_matrix(first, second):
    size = first * second
    row = lax.broadcasted_iota(jnp.int32, (size, size), 0)
    column = lax.broadcasted_iota(jnp.int32, (size, size), 1)
    return ((row % second) * first + row // second == column).astype(jnp.bfloat16)


def swap_rows(blocks):
    first, second, width = blocks.shape
    swapped = jnp.dot(
        swap_matrix(second, first),
        blocks.reshape(first * second, width),
        preferred_element_type=jnp.float32,
    )
    return swapped.astype(jnp.bfloat16).reshape(second, first, width)


def attend(queries, cached, fresh, lengths):
    steps, rows, query_width = queries.shape
    context = cached.shape[1]
    width = cached.shape[2] // 2
    group = query_width // width
    pages = jnp.concatenate(
        [cached.reshape(rows * context, 2 * width), fresh.reshape(steps * rows, 2 * width)], axis=0
    )
    query = jnp.concatenate(
        [queries[s, :, g * width : (g + 1) * width] for s in range(steps) for g in range(group)],
        axis=0,
    )
    scores = lax.dot_general(
        query, pages[:, :width], (((1,), (1,)), ((), ())), preferred_element_type=jnp.float32
    ) * (width ** (-0.5))
    asking = lax.broadcasted_iota(jnp.int32, scores.shape, 0)
    asked = lax.broadcasted_iota(jnp.int32, scores.shape, 1)
    own, step = asking % rows, asking // (group * rows)
    new = asked - rows * context
    cache_live = (new < 0) & (asked // context == own) & (asked % context < lengths)
    fresh_live = (new >= 0) & (new % rows == own) & (new // rows <= step)
    live = cache_live | fresh_live
    top = jnp.max(jnp.where(live, scores, -1e30), axis=-1, keepdims=True)
    raised = jnp.where(live, jnp.exp(scores - top), 0.0)
    weights = (raised / jnp.sum(raised, axis=-1, keepdims=True)).astype(jnp.bfloat16)
    summed = jnp.dot(weights, pages[:, width:], preferred_element_type=jnp.float32)
    summed = summed.astype(jnp.bfloat16)
    return [
        [summed[(s * group + g) * rows : (s * group + g + 1) * rows] for g in range(group)]
        for s in range(steps)
    ]


def grow(cached, fresh, lengths):
    rows, context, width = cached.shape
    steps = fresh.shape[0]
    shape = (rows * context, steps * rows)
    place = lax.broadcasted_iota(jnp.int32, shape, 0)
    token = lax.broadcasted_iota(jnp.int32, shape, 1)
    hit = (place // context == token % rows) & (place % context == lengths + token // rows)
    chosen = jnp.dot(
        hit.astype(jnp.bfloat16),
        fresh.reshape(steps * rows, width),
        preferred_element_type=jnp.float32,
    )
    written = jnp.max(hit.astype(jnp.float32), axis=1, keepdims=True) > 0.0
    kept = cached.reshape(rows * context, width).astype(jnp.float32)
    shape = (steps * rows, steps * rows)
    place = lax.broadcasted_iota(jnp.int32, shape, 0)
    token = lax.broadcasted_iota(jnp.int32, shape, 1)
    hit = (place % rows == token % rows) & (context + place // rows == lengths + token // rows)
    tail = jnp.dot(
        hit.astype(jnp.bfloat16),
        fresh.reshape(steps * rows, width),
        preferred_element_type=jnp.float32,
    )
    grown = jnp.where(written, chosen, kept).astype(jnp.bfloat16)
    return grown.reshape(rows, context, width), tail.astype(jnp.bfloat16).reshape(steps, rows, width)


def move_kernel(
    lengths,
    destination,
    mamba_in,
    xproj_in,
    cached_in,
    fresh_in,
    queries_in,
    dtproj_in,
    bias_in,
    a_log_in,
    skip_in,
    state_in,
    out_early,
    out_late,
    mamba_rows,
    xproj,
    cached,
    fresh,
    queries,
    dtproj,
    bias,
    a_log,
    skip,
    state,
    part,
    arrived,
    total,
    decay_rate,
    step_size,
    drive,
    b_wide,
    c_wide,
    readout,
    early,
    late,
    mamba,
    bundles_early,
    bundles_late,
    table,
    chosen,
    tables_come,
    tables,
    loaded,
    sum_sent,
    sum_come,
    total_sent,
    total_come,
    table_sent,
    table_come,
    table_kept,
    first_sent,
    first_come,
    sent,
    come,
    kept,
    *blocks,
):
    me = lax.axis_index("replica")
    shard = lax.axis_index("tensor")
    shards = lax.axis_size("tensor")
    place = (me // SIDE, me % SIDE)
    ahead = 1 - 2 * lax.rem(shard, 2)

    def device(route, first, second):
        return (first * SIDE + second if route == 0 else second * SIDE + first, shard)

    def along(route, hop):
        return lax.rem(place[route] + hop * ahead + SIDE, SIDE)

    barrier = pltpu.get_barrier_semaphore()
    for hop in range(1, shards):
        peer = (me, lax.rem(shard + hop, shards))
        pl.semaphore_signal(barrier, inc=1, device_id=peer, device_id_type=MESH)
    for route in range(2):
        for hop in NEAR_FIRST:
            peer = device(route, lax.rem(place[route] + hop, SIDE), place[1 - route])
            pl.semaphore_signal(barrier, inc=1, device_id=peer, device_id_type=MESH)

    loads = [
        pltpu.make_async_copy(source, held, loaded.at[index])
        for index, (source, held) in enumerate(
            [
                (mamba_in, mamba_rows),
                (xproj_in, xproj),
                (cached_in, cached),
                (fresh_in, fresh),
                (queries_in, queries),
                (dtproj_in, dtproj),
                (bias_in, bias),
                (a_log_in, a_log),
                (skip_in, skip),
                (state_in, state),
            ]
        )
    ]
    for load in loads:
        load.start()

    steps, _, rows, width = mamba.shape
    sources = (early, late)
    bundles = (bundles_early, bundles_late)
    outs = (out_early, out_late)
    hops = len(BLOCK_HOPS)

    def block_of(stage, route, which):
        return blocks[(stage * 2 + route) * hops + which]

    for stage in range(2):
        for route in range(2):
            for which in range(hops):
                block = block_of(stage, route, which)
                block[rows] = jnp.zeros(block.shape[1:], block.dtype)
    for route in range(2):
        early[route, rows] = jnp.zeros(early.shape[2:], early.dtype)
        late[route, rows] = jnp.zeros(late.shape[2:], late.dtype)
    slot_id = lax.broadcasted_iota(jnp.int32, table.shape, 1)
    slot_row = jnp.full(table.shape, rows, jnp.int32)
    for row in range(rows):
        slot_row = jnp.where(slot_id == destination[row], row, slot_row)
    table[...] = slot_row
    keep_own = pltpu.make_async_copy(table, chosen, table_kept.at[0])
    keep_own.start()

    started = []

    def ship(source, target, stage, route, which, step):
        copy = pltpu.make_async_remote_copy(
            src_ref=source,
            dst_ref=target,
            send_sem=first_sent.at[stage, route, which],
            recv_sem=first_come.at[stage, route, which],
            device_id=device(route, along(route, step), place[1 - route]),
            device_id_type=MESH,
        )
        copy.start()
        started.append(copy)
        return copy

    def select(stage, route, block, slots, first, kind):
        def one(second, unused):
            slot = first * SIDE + second if route == 0 else second * SIDE + first
            bundles[stage][route, kind, second] = block[slots(slot)]
            return unused

        lax.fori_loop(0, SIDE, one, 0)

    def pass_on(stage, route, kind, hop):
        mine = place[1 - route]
        origin = along(route, -hop)
        pair = (origin, mine) if route == 0 else (mine, origin)
        slot = outs[stage].at[route, pair[0], pair[1]]
        for step in NEAR_FIRST:
            target = lax.rem(mine + step, SIDE)
            pltpu.make_async_remote_copy(
                src_ref=bundles[stage].at[route, kind, target],
                dst_ref=slot,
                send_sem=sent.at[stage],
                recv_sem=come.at[stage],
                device_id=device(route, place[route], target),
                device_id_type=MESH,
            ).start()
        pltpu.make_async_copy(
            bundles[stage].at[route, kind, mine], slot, kept.at[stage]
        ).start()

    def pass_own(stage):
        for route in range(2):
            block = sources[stage].at[route]
            select(stage, route, block, lambda slot: chosen[0, slot], place[route], 0)
            pass_on(stage, route, 0, 0)

    def pass_block(stage, route, which):
        select(
            stage,
            route,
            block_of(stage, route, which),
            lambda slot: tables[route, which, 0, slot],
            place[route],
            1 + which,
        )
        pass_on(stage, route, 1 + which, BLOCK_HOPS[which])

    legs = {}

    def start_block(stage, route, which, source, step):
        target = block_of(stage, route, which).at[pl.ds(0, rows)]
        legs[stage, route, which] = ship(
            source.at[pl.ds(0, rows)], target, stage, route, which, step
        )

    def start_bundle(stage, route, which, kind, step):
        select(
            stage,
            route,
            block_of(stage, route, which),
            lambda slot: tables[route, which, 0, slot],
            along(route, step),
            kind,
        )
        held = bundles[stage]
        legs[stage, route, kind] = ship(
            held.at[route, kind], held.at[route, kind + 2], stage, route, kind, step
        )

    def first_leg(stage, route):
        start_block(stage, route, 0, sources[stage].at[route], 1)
        start_block(stage, route, 3, sources[stage].at[route], -1)

    def second_leg(stage):
        for route in range(2):
            legs[stage, route, 0].wait_recv()
            start_block(stage, route, 1, block_of(stage, route, 0), 1)
            legs[stage, route, 3].wait_recv()
            start_block(stage, route, 4, block_of(stage, route, 3), -1)
        for route in range(2):
            pass_block(stage, route, 0)
            pass_block(stage, route, 3)

    def third_leg(stage):
        for route in range(2):
            legs[stage, route, 1].wait_recv()
            start_block(stage, route, 2, block_of(stage, route, 1), 1)
            legs[stage, route, 4].wait_recv()
            start_bundle(stage, route, 4, 6, -1)
        for route in range(2):
            pass_block(stage, route, 1)
            pass_block(stage, route, 4)

    def fourth_leg(stage):
        for route in range(2):
            legs[stage, route, 2].wait_recv()
            start_bundle(stage, route, 2, 7, 1)
        for route in range(2):
            pass_block(stage, route, 2)
            legs[stage, route, 6].wait_recv()
            pass_on(stage, route, 8, -3)

    def last_leg(stage):
        for route in range(2):
            legs[stage, route, 7].wait_recv()
            pass_on(stage, route, 9, 4)

    loads[0].wait()
    for step in range(steps):
        for kind in range(2):
            mamba[step, kind] = mamba_rows[:, step, kind].astype(jnp.float32).astype(jnp.bfloat16)
    loads[1].wait()
    chunk = part.shape[1]
    per_step = rows // chunk
    for step in range(steps):
        block = lax.dot_general(
            mamba[step, 0],
            xproj[...],
            (((1,), (1,)), ((), ())),
            preferred_element_type=jnp.float32,
        )
        for piece in range(per_step):
            part[step * per_step + piece] = block[piece * chunk : (piece + 1) * chunk]
    for piece in range(steps * per_step, shards):
        part[piece] = jnp.zeros(part.shape[1:], part.dtype)
    keep_own.wait()
    pl.semaphore_wait(barrier, shards - 1 + 2 * len(NEAR_FIRST))

    sums = []
    for hop in range(1, shards):
        target = lax.rem(shard + hop, shards)
        copy = pltpu.make_async_remote_copy(
            src_ref=part.at[target],
            dst_ref=arrived.at[hop],
            send_sem=sum_sent.at[hop],
            recv_sem=sum_come.at[hop],
            device_id=(me, target),
            device_id_type=MESH,
        )
        copy.start()
        sums.append(copy)
    table_legs = []
    for which, hop in enumerate(BLOCK_HOPS):
        for route in range(2):
            copy = pltpu.make_async_remote_copy(
                src_ref=table,
                dst_ref=tables_come.at[route, which],
                send_sem=table_sent.at[route, which],
                recv_sem=table_come.at[route, which],
                device_id=device(route, along(route, hop), place[1 - route]),
                device_id_type=MESH,
            )
            copy.start()
            table_legs.append(copy)

    context, page_width = cached.shape[1:]
    token = lax.broadcasted_iota(jnp.int32, (1, steps * rows), 1)
    asked = lax.broadcasted_iota(jnp.int32, (1, rows * context + steps * rows), 1)
    key_row = jnp.where(asked < rows * context, asked // context, (asked - rows * context) % rows)
    key_lengths = jnp.zeros_like(asked)
    token_lengths = jnp.zeros_like(token)
    for row in range(rows):
        key_lengths = jnp.where(key_row == row, lengths[row], key_lengths)
        token_lengths = jnp.where(token % rows == row, lengths[row], token_lengths)
    for load in loads[2:5]:
        load.wait()
    grown, tail = grow(cached[...], fresh[...], token_lengths)
    early[0, :rows] = grown
    first_leg(0, 0)
    attended = attend(queries[...], cached[...], fresh[...], key_lengths)
    per_block = page_width // 128
    pieces = [tail[step] for step in range(steps)]
    for step in range(steps):
        for g in range(0, len(attended[step]), per_block):
            pieces.append(jnp.concatenate(attended[step][g : g + per_block], axis=1))
    while len(pieces) < early.shape[2]:
        pieces.append(jnp.zeros((rows, page_width), jnp.bfloat16))
    early[1, :rows] = swap_rows(jnp.stack(pieces))
    first_leg(0, 1)
    pass_own(0)
    for load in loads[5:]:
        load.wait()
    decay_rate[...] = -jnp.exp(a_log[...])

    summed = part[shard]
    for hop in range(1, shards):
        sums[hop - 1].wait_recv()
        summed = summed + arrived[hop]
    total[shard] = summed
    totals = []
    for hop in range(1, shards):
        target = lax.rem(shard + hop, shards)
        copy = pltpu.make_async_remote_copy(
            src_ref=total.at[shard],
            dst_ref=total.at[shard],
            send_sem=total_sent.at[hop],
            recv_sem=total_come.at[hop],
            device_id=(me, target),
            device_id_type=MESH,
        )
        copy.start()
        totals.append(copy)
    for copy in table_legs:
        copy.wait_recv()
    keep = pltpu.make_async_copy(tables_come, tables, table_kept.at[1])
    keep.start()
    keep.wait()
    second_leg(0)
    for copy in totals:
        copy.wait_recv()

    low_width = dtproj.shape[0]
    state_size = a_log.shape[0]
    lane = 128
    projected = total[...].reshape(shards * chunk, total.shape[2])[: steps * rows]
    low_rank = projected[:, :low_width].astype(jnp.bfloat16)
    raw = jnp.dot(low_rank, dtproj[...], preferred_element_type=jnp.float32) + bias[...]
    step_size[...] = jnp.maximum(raw, 0.0) + jnp.log1p(jnp.exp(-jnp.abs(raw)))
    for step in range(steps):
        span = slice(step * rows, (step + 1) * rows)
        drive[span] = step_size[span] * mamba[step, 0].astype(jnp.float32)
    turned = jnp.transpose(projected[:, low_width:])
    for index in range(steps * rows):
        column = turned[:, index : index + 1]
        b_wide[index] = jnp.broadcast_to(column[:state_size], (state_size, lane))
        c_wide[index] = jnp.broadcast_to(column[state_size:], (state_size, lane))

    cut = late.shape[3]
    rest = width - cut

    def update(route, skipped):
        def one(piece, unused):
            span = pl.ds(pl.multiple_of(piece * lane + skipped, lane), lane)
            goal = pl.ds(pl.multiple_of(piece * lane, lane), lane)
            rate = decay_rate[:, span]
            for row in range(rows):
                carry = state[row, :, span]
                for step in range(steps):
                    index = step * rows + row
                    size = step_size[index : index + 1, span]
                    carry = (
                        jnp.exp(size * rate) * carry
                        + b_wide[index] * drive[index : index + 1, span]
                    )
                    readout[index : index + 1, span] = jnp.sum(
                        c_wide[index] * carry, axis=0, keepdims=True
                    )
                late[route, row, :, goal] = carry.astype(jnp.bfloat16)
            return unused

        return one

    third_leg(0)
    lax.fori_loop(0, cut // lane, update(0, 0), 0)
    first_leg(1, 0)
    lax.fori_loop(0, rest // lane, update(1, cut), 0)
    pieces = []
    for step in range(steps):
        x = mamba[step, 0].astype(jnp.float32)
        z = mamba[step, 1].astype(jnp.float32)
        whole = readout[step * rows : (step + 1) * rows] + skip[...] * x
        mixed = (whole * (z / (1.0 + jnp.exp(-z)))).astype(jnp.bfloat16)
        for start in range(0, width, page_width):
            pieces.append(mixed[:, start : start + page_width])
    while len(pieces) < state_size:
        pieces.append(jnp.zeros((rows, page_width), jnp.bfloat16))
    late[1, :rows, :, rest:] = swap_rows(jnp.stack(pieces))

    first_leg(1, 1)
    pass_own(1)
    fourth_leg(0)
    second_leg(1)
    last_leg(0)
    third_leg(1)
    fourth_leg(1)
    last_leg(1)

    for copy in table_legs + sums + totals + started:
        copy.wait_send()
    for stage in range(2):
        others = outs[stage].at[:, :, pl.ds(0, SIDE - 1)]
        own = outs[stage].at[:, :, 0]
        pltpu.make_async_copy(own, own, kept.at[stage]).wait()
        pltpu.make_async_copy(others, others, sent.at[stage]).wait()
        pltpu.make_async_copy(others, others, come.at[stage]).wait()


def move_rows(lengths, destination, *arrays):
    mamba, xproj_w, cached, a_log = arrays[0], arrays[1], arrays[2], arrays[7]
    rows, steps, _, width = mamba.shape
    state_size = a_log.shape[0]
    page_width = cached.shape[2]
    half = (width + page_width) // 2
    shards = lax.axis_size("tensor")
    grid = (2, SIDE, SIDE, state_size)
    kinds = (2, 10, SIDE, state_size)
    early_grid, late_grid = grid + (page_width,), grid + (half,)
    sums = (shards, steps * rows // 6, xproj_w.shape[0])
    table = (1, 2 * SIDE * SIDE)
    tables = (2, len(BLOCK_HOPS)) + table
    early_block = pltpu.VMEM((rows + 1, state_size, page_width), jnp.bfloat16)
    late_block = pltpu.VMEM((rows + 1, state_size, half), jnp.bfloat16)
    blocks = [early_block] * (2 * len(BLOCK_HOPS)) + [late_block] * (2 * len(BLOCK_HOPS))
    outs = pl.pallas_call(
        move_kernel,
        out_shape=(
            jax.ShapeDtypeStruct(early_grid, jnp.bfloat16),
            jax.ShapeDtypeStruct(late_grid, jnp.bfloat16),
        ),
        in_specs=[
            pl.BlockSpec(memory_space=pltpu.SMEM),
            pl.BlockSpec(memory_space=pltpu.SMEM),
        ]
        + [pl.BlockSpec(memory_space=pl.ANY)] * len(arrays),
        out_specs=(pl.BlockSpec(memory_space=pl.ANY), pl.BlockSpec(memory_space=pl.ANY)),
        scratch_shapes=[pltpu.VMEM(array.shape, array.dtype) for array in arrays]
        + [pltpu.VMEM(sums, jnp.float32)] * 3
        + [
            pltpu.VMEM((state_size, width), jnp.float32),
            pltpu.VMEM((steps * rows, width), jnp.float32),
            pltpu.VMEM((steps * rows, width), jnp.float32),
            pltpu.VMEM((steps * rows, state_size, 128), jnp.float32),
            pltpu.VMEM((steps * rows, state_size, 128), jnp.float32),
            pltpu.VMEM((steps * rows, width), jnp.float32),
            pltpu.VMEM((2, rows + 1, state_size, page_width), jnp.bfloat16),
            pltpu.VMEM((2, rows + 1, state_size, half), jnp.bfloat16),
            pltpu.VMEM((steps, 2, rows, width), jnp.bfloat16),
            pltpu.VMEM(kinds + (page_width,), jnp.bfloat16),
            pltpu.VMEM(kinds + (half,), jnp.bfloat16),
            pltpu.VMEM(table, jnp.int32),
            pltpu.SMEM(table, jnp.int32),
            pltpu.VMEM(tables, jnp.int32),
            pltpu.SMEM(tables, jnp.int32),
            pltpu.SemaphoreType.DMA((len(arrays),)),
        ]
        + [pltpu.SemaphoreType.DMA((shards,))] * 4
        + [pltpu.SemaphoreType.DMA((2, len(BLOCK_HOPS)))] * 2
        + [pltpu.SemaphoreType.DMA((2,))]
        + [pltpu.SemaphoreType.DMA((2, 2, SIDE))] * 2
        + [pltpu.SemaphoreType.DMA((2,))] * 3
        + blocks,
        name="move_rows",
        compiler_params=pltpu.CompilerParams(
            collective_id=1, has_side_effects=True, vmem_limit_bytes=60 << 20
        ),
    )(lengths, destination, *arrays)
    return [out.reshape((2, SIDE * SIDE) + out.shape[3:]) for out in outs]


def unpack_kernel(
    early_in,
    late_in,
    mixed_out,
    attended_out,
    state_out,
    pages_out,
    early,
    late,
    mixed,
    attended,
    pages,
    come,
    gone,
):
    steps, slots, width = mixed.shape
    page_width = pages.shape[2]
    cut = late.shape[3]
    left = width - cut
    context = early.shape[2]
    per_step = width // page_width
    block = 16
    loads = []
    for index in range(slots // block):
        span = pl.ds(index * block, block)
        group = []
        for route in range(2):
            for kind, (source, held) in enumerate([(late_in, late), (early_in, early)]):
                copy = pltpu.make_async_copy(
                    source.at[route, span], held.at[route, span], come.at[index, 2 * route + kind]
                )
                copy.start()
                group.append(copy)
        loads.append(group)
    stores = []

    def store(source, goal, index, which):
        copy = pltpu.make_async_copy(source, goal, gone.at[index, which])
        copy.start()
        stores.append(copy)

    for index, group in enumerate(loads):
        for copy in group:
            copy.wait()
        span = pl.ds(index * block, block)
        rows = slice(index * block, (index + 1) * block)
        store(late.at[0, span], state_out.at[span, :, pl.ds(0, cut)], index, 0)
        store(
            late.at[1, span, :, pl.ds(0, left)], state_out.at[span, :, pl.ds(cut, left)], index, 1
        )
        pages[:context, rows] = swap_rows(early[0, rows])
        swapped = swap_rows(early[1, rows])
        pages[context:, rows] = swapped[:steps]
        store(pages.at[:, span], pages_out.at[:, span], index, 2)
        for step in range(steps):
            for piece in range(per_step):
                lanes = slice(piece * page_width, (piece + 1) * page_width)
                attended[step, rows, lanes] = swapped[steps + step * per_step + piece]
        store(attended.at[:, span], attended_out.at[:, span], index, 3)
        swapped = swap_rows(late[1, rows, :, left:])
        for step in range(steps):
            for piece in range(per_step):
                lanes = slice(piece * page_width, (piece + 1) * page_width)
                mixed[step, rows, lanes] = swapped[step * per_step + piece]
        store(mixed.at[:, span], mixed_out.at[:, span], index, 4)
    for copy in stores:
        copy.wait()


def unpack(early, late, steps, width):
    _, slots, state_size, page_width = early.shape
    wide = (steps, slots, width)
    paged = (state_size + steps, slots, page_width)
    return pl.pallas_call(
        unpack_kernel,
        out_shape=(
            jax.ShapeDtypeStruct(wide, jnp.bfloat16),
            jax.ShapeDtypeStruct(wide, jnp.bfloat16),
            jax.ShapeDtypeStruct((slots, state_size, width), jnp.bfloat16),
            jax.ShapeDtypeStruct(paged, jnp.bfloat16),
        ),
        in_specs=[pl.BlockSpec(memory_space=pl.ANY)] * 2,
        out_specs=(pl.BlockSpec(memory_space=pl.ANY),) * 4,
        scratch_shapes=[
            pltpu.VMEM(early.shape, jnp.bfloat16),
            pltpu.VMEM(late.shape, jnp.bfloat16),
            pltpu.VMEM(wide, jnp.bfloat16),
            pltpu.VMEM(wide, jnp.bfloat16),
            pltpu.VMEM(paged, jnp.bfloat16),
            pltpu.SemaphoreType.DMA((slots // 16, 4)),
            pltpu.SemaphoreType.DMA((slots // 16, 5)),
        ],
        name="unpack",
        compiler_params=pltpu.CompilerParams(vmem_limit_bytes=60 << 20),
    )(early, late)


def per_device(
    mamba_in,
    queries,
    new_kv,
    ssm_state,
    kv_cache,
    lengths,
    destination,
    xproj_w,
    dtproj_w,
    dt_bias,
    a_log,
    d_skip,
):
    steps, width = mamba_in.shape[1], mamba_in.shape[3]
    early, late = move_rows(
        lengths,
        destination[:, 0],
        mamba_in,
        xproj_w.T,
        kv_cache[:, :, 0],
        jnp.transpose(new_kv[:, :, 0], (1, 0, 2)),
        jnp.transpose(queries[:, :, 0], (1, 0, 2)),
        dtproj_w,
        dt_bias[None],
        a_log,
        d_skip[None],
        ssm_state,
    )
    mixed, attended, state, pages = unpack(early, late, steps, width)
    return (
        jnp.transpose(mixed, (1, 0, 2)),
        jnp.transpose(attended, (1, 0, 2))[:, :, None],
        state,
        jnp.transpose(pages, (1, 0, 2))[:, :, None],
    )


def solution(mesh):
    placed = (
        P("replica", None, None, "tensor"),
        P("replica", None, "tensor", None),
        P("replica", None, "tensor", None),
        P("replica", None, "tensor"),
        P("replica", None, "tensor", None),
        P("replica"),
        P("replica", None),
        P("tensor", None),
        P(None, "tensor"),
        P("tensor"),
        P(None, "tensor"),
        P("tensor"),
    )
    return jax.shard_map(
        per_device,
        mesh=mesh,
        in_specs=placed,
        out_specs=(
            P("replica", None, "tensor"),
            P("replica", None, "tensor", None),
            P("replica", None, "tensor"),
            P("replica", None, "tensor", None),
        ),
        check_vma=False,
    )
```
